512 devices in a mesh: gx: 32 (over z, core), gy: 16 (over x, y).
Axes of the slice: x: 4, y: 4, z: 16, core: 2. Of those that a mesh axis runs over, the one named last changes fastest.
Arguments:
- features: float32 [32, 16, 128, 256], P('gx', 'gy'), may hold values from -6 to 6
- offsets: float32 [32, 16, 3, 128], P('gx', 'gy'), may hold values from 0 to 1
- species: int32 [32, 16, 128], P('gx', 'gy'), may hold values from 0 to 63
- neighbours: int32 [32, 16, 128, 8], P('gx', 'gy'), may hold values from 0 to 65535, as said below
- edge_mask: int32 [32, 16, 128, 8], P('gx', 'gy'), may hold values 0 or 1
- wavevectors: int32 [3, 512], replicated, may hold values from -16 to 15, as said below
- value_weight: float32 [256, 256], replicated, may hold values from -0.375 to 0.375
- radial_weight: float32 [64, 256], replicated, may hold values from -3 to 3
- species_embed: float32 [64, 256], replicated, may hold values from -3 to 3
- mixing_weight: float32 [256, 256], replicated, may hold values from -0.375 to 0.375
- group_filter: float32 [32, 256, 256], P('gx'), may hold values from -0.375 to 0.375
Outputs:
- updated: float32 [32, 16, 128, 256], P('gx', 'gy')
The draws below stay inside these ranges and needn't reach their ends.
Inputs may be any that keep to these rules, and one draw needn't show every extreme that they name: `neighbours`: every listed neighbour lies in a block whose first index differs from the atom's by at most one modulo 32 and whose second index differs by at most one modulo 16. `wavevectors`: the first component lies in -16 .. 15, the second in -8 .. 7, the third in -2 .. 2.
All inputs are finite; a program needn't handle non-finite values. No bound on the sum of `edge_mask` on one device may be relied on, other than what follows from the above.
Results may differ from the reference program's by a relative error of at most 0.0003.
Values sent between devices are 32-bit elements; how exact they have to be, the bound alone decides.
A program may use at most 64 MiB of HBM per device.

```python
import math
import jax
import jax.numpy as jnp
from jax import lax

CHANNELS = 256
RADIAL = 64
SPECIES = 64
NEIGHBOUR_SLOTS = 8
MODE_COUNT = 512
ATOM_DEV = 128
LATERAL_BLOCKS = 32
TRANSVERSE_BLOCKS = 16
GROUPS = 32
GROUP_MODES = 16
ATOM_COUNT = 65536


def draw_neighbours(key, part):
    lateral_key, transverse_key, atom_key = jax.random.split(key, 3)
    shape = (LATERAL_BLOCKS, TRANSVERSE_BLOCKS, ATOM_DEV, NEIGHBOUR_SLOTS)
    lateral_shift = jax.random.randint(lateral_key, shape, -1, 2)
    transverse_shift = jax.random.randint(transverse_key, shape, -1, 2)
    chosen = jax.random.randint(atom_key, shape, 0, ATOM_DEV)
    lateral_block = jnp.arange(LATERAL_BLOCKS, dtype=jnp.int32)[:, None, None, None]
    transverse_block = jnp.arange(TRANSVERSE_BLOCKS, dtype=jnp.int32)[None, :, None, None]
    source_lateral = jnp.remainder(lateral_block + lateral_shift, LATERAL_BLOCKS)
    source_transverse = jnp.remainder(transverse_block + transverse_shift, TRANSVERSE_BLOCKS)
    return ((source_lateral * TRANSVERSE_BLOCKS + source_transverse) * ATOM_DEV + chosen).astype(jnp.int32)


def draw_wavevectors(key, part):
    lateral_key, transverse_key, vertical_key = jax.random.split(key, 3)
    lateral_half = LATERAL_BLOCKS // 2
    transverse_half = TRANSVERSE_BLOCKS // 2
    lateral_part = jax.random.randint(lateral_key, (MODE_COUNT,), -lateral_half, lateral_half)
    transverse_part = jax.random.randint(transverse_key, (MODE_COUNT,), -transverse_half, transverse_half)
    vertical_part = jax.random.randint(vertical_key, (MODE_COUNT,), -2, 3)
    return jnp.stack([lateral_part, transverse_part, vertical_part]).astype(jnp.int32)


def set_ends(entries, rng, low, top_value):
    place = [jax.random.randint(jax.random.fold_in(rng, axis), (), 0, length) for axis, length in enumerate(entries.shape)]
    widest = entries.shape.index(max(entries.shape))
    beside = place[:widest] + [(place[widest] + 1) % entries.shape[widest]] + place[widest + 1:]
    return entries.at[tuple(place)].set(low).at[tuple(beside)].set(top_value)


def steps_of(own_key, extent, cuts, low, top_value):
    def one(dim, shards_of):
        draws = jax.random.uniform(jax.random.fold_in(jax.random.fold_in(own_key, 6), dim), (shards_of,), jnp.float32, low / len(cuts), top_value / len(cuts))
        return jnp.repeat(jnp.exp(draws), extent[dim] // shards_of).reshape((-1,) + (1,) * (len(extent) - dim - 1))

    gain = one(*cuts[0])
    for cut in cuts[1:]:
        gain = gain * one(*cut)
    return gain


def gaussian(key, shape, deviation, limit, pieces=(), kind=jnp.bfloat16):
    result = jax.random.normal(key, shape, jnp.float32) * deviation
    if len(pieces) > 0:
        result = steps_of(key, shape, pieces, -0.22, 0.18) * result
    return jnp.clip(result, min=-limit, max=limit).astype(kind)


def setup_inputs(seed: int = 0) -> dict:
    keys = jax.random.split(jax.random.key(seed), 12)
    features = gaussian(keys[0], (LATERAL_BLOCKS, TRANSVERSE_BLOCKS, ATOM_DEV, CHANNELS), 1.0, 6.0, ((0, 32), (1, 16)), jnp.float32)
    offsets = jnp.clip(1.0 * jax.random.uniform(keys[1], (LATERAL_BLOCKS, TRANSVERSE_BLOCKS, 3, ATOM_DEV), jnp.float32) ** steps_of(keys[1], (LATERAL_BLOCKS, TRANSVERSE_BLOCKS, 3, ATOM_DEV), ((0, 32), (1, 16)), -0.2, 0.2), 0.0, 1.0)
    species = set_ends(jax.random.randint(keys[2], (LATERAL_BLOCKS, TRANSVERSE_BLOCKS, ATOM_DEV), 0, SPECIES), jax.random.fold_in(keys[2], 1), 0, SPECIES - 1).astype(jnp.int32)
    neighbours = draw_neighbours(jax.random.fold_in(keys[11], 71), 0)
    edge_mask = set_ends((jax.random.randint(keys[4], (LATERAL_BLOCKS, TRANSVERSE_BLOCKS, ATOM_DEV, NEIGHBOUR_SLOTS), 0, 4) < 3).astype(jnp.int32), jax.random.fold_in(keys[4], 1), 0, 1)
    wavevectors = draw_wavevectors(jax.random.fold_in(keys[11], 71), 0)
    value_weight = gaussian(keys[6], (CHANNELS, CHANNELS), CHANNELS ** -0.5, 0.375, (), jnp.float32)
    radial_weight = gaussian(keys[7], (RADIAL, CHANNELS), 4 ** -0.5, 3.0, (), jnp.float32)
    species_embed = gaussian(keys[8], (SPECIES, CHANNELS), 0.5, 3.0, (), jnp.float32)
    mixing_weight = gaussian(keys[9], (CHANNELS, CHANNELS), CHANNELS ** -0.5, 0.375, (), jnp.float32)
    group_filter = gaussian(keys[10], (GROUPS, CHANNELS, CHANNELS), CHANNELS ** -0.5, 0.375, ((0, 32),), jnp.float32)
    return {"features": features, "offsets": offsets, "species": species, "neighbours": neighbours, "edge_mask": edge_mask, "wavevectors": wavevectors, "value_weight": value_weight, "radial_weight": radial_weight, "species_embed": species_embed, "mixing_weight": mixing_weight, "group_filter": group_filter}


FULL_TURN = 2.0 * math.pi
SMEARING = 0.01
RADIAL_REACH = 3.0
SOFTEN = 0.01
HIGHEST = lax.Precision.HIGHEST

def radial(distance, basis_count):
    centres = jnp.arange(basis_count, dtype=jnp.float32) * (RADIAL_REACH / (basis_count - 1))
    spread = 2.0 * RADIAL_REACH / (basis_count - 1)
    scaled = (distance[..., None] - centres) / spread
    return jnp.exp(-scaled * scaled)

def phase_table(vectors, lateral_block, transverse_block, offsets_block, lateral_span, transverse_span):
    weights = vectors.astype(jnp.float32)
    lateral_whole = jnp.remainder(vectors[0] * lateral_block, lateral_span).astype(jnp.float32)
    transverse_whole = jnp.remainder(vectors[1] * transverse_block, transverse_span).astype(jnp.float32)
    fractions = (lateral_whole[None, :] + offsets_block[0][:, None] * weights[0][None, :]) / lateral_span
    fractions = fractions + (transverse_whole[None, :] + offsets_block[1][:, None] * weights[1][None, :]) / transverse_span
    fractions = fractions + offsets_block[2][:, None] * weights[2][None, :]
    return FULL_TURN * fractions

def damping(vectors, lateral_span, transverse_span):
    weights = vectors.astype(jnp.float32)
    lateral_wave = FULL_TURN * weights[0] / lateral_span
    transverse_wave = FULL_TURN * weights[1] / transverse_span
    vertical_wave = FULL_TURN * weights[2]
    return jnp.exp(-SMEARING * (lateral_wave * lateral_wave + transverse_wave * transverse_wave + vertical_wave * vertical_wave))

def edge_messages(nearby_values, nearby_offsets, own_position, lateral_shift, transverse_shift, keep_mask, own_embed, nearby_embed, radial_weight, mixing_weight):
    lateral_gap = lateral_shift.astype(jnp.float32) + nearby_offsets[..., 0] - own_position[:, None, 0]
    transverse_gap = transverse_shift.astype(jnp.float32) + nearby_offsets[..., 1] - own_position[:, None, 1]
    vertical_gap = nearby_offsets[..., 2] - own_position[:, None, 2]
    distance = jnp.sqrt(lateral_gap * lateral_gap + transverse_gap * transverse_gap + vertical_gap * vertical_gap + SOFTEN)
    basis = radial(distance, radial_weight.shape[0])
    basis_rows = basis.reshape(-1, basis.shape[-1])
    before = jnp.dot(basis_rows, radial_weight, precision=HIGHEST, preferred_element_type=jnp.float32).reshape(nearby_values.shape)
    hidden = jax.nn.silu(before + own_embed[:, None, :] + nearby_embed)
    filters = jnp.dot(hidden.reshape(-1, hidden.shape[-1]), mixing_weight, precision=HIGHEST, preferred_element_type=jnp.float32).reshape(nearby_values.shape)
    messages = filters * nearby_values * keep_mask.astype(jnp.float32)[..., None]
    return lax.optimization_barrier(jnp.sum(messages, axis=1)) / math.sqrt(nearby_values.shape[1])

def contract_atoms(table, feats):
    return lax.dot_general(table, feats, (((0,), (0,)), ((), ())), precision=HIGHEST, preferred_element_type=jnp.float32)

def reference(features, offsets, species, neighbours, edge_mask, wavevectors, value_weight, radial_weight, species_embed, mixing_weight, group_filter):
    lateral_span = LATERAL_BLOCKS
    transverse_span = TRANSVERSE_BLOCKS
    block_total = lateral_span * transverse_span
    channel_count = features.shape[-1]
    block_features = features.reshape(block_total, ATOM_DEV, channel_count)
    block_offsets = offsets.reshape(block_total, 3, ATOM_DEV)
    block_species = species.reshape(block_total, ATOM_DEV)
    block_neighbours = neighbours.reshape(block_total, ATOM_DEV, NEIGHBOUR_SLOTS)
    block_masks = edge_mask.reshape(block_total, ATOM_DEV, NEIGHBOUR_SLOTS)
    values = jnp.dot(features.reshape(-1, channel_count), value_weight, precision=HIGHEST, preferred_element_type=jnp.float32)
    positions = jnp.transpose(block_offsets, (0, 2, 1)).reshape(-1, 3)
    atom_embed = species_embed[species.reshape(-1)]
    block_index = jnp.arange(block_total, dtype=jnp.int32)

    def accumulate(running, inputs):
        which, feats, offsets_block = inputs
        angles = phase_table(wavevectors, which // transverse_span, which % transverse_span, offsets_block, lateral_span, transverse_span)
        partial_sum = jnp.concatenate([contract_atoms(jnp.cos(angles), feats), contract_atoms(jnp.sin(angles), feats)], axis=1)
        return (running + partial_sum, None)
    structure, unused = lax.scan(accumulate, jnp.zeros((MODE_COUNT, 2 * channel_count), jnp.float32), (block_index, block_features, block_offsets))
    grouped = structure.reshape(GROUPS, GROUP_MODES, 2, channel_count)
    mixed = jnp.einsum('gmcf,gfh->gmch', grouped, group_filter, precision=HIGHEST, preferred_element_type=jnp.float32)
    filtered = damping(wavevectors, lateral_span, transverse_span)[:, None] * mixed.reshape(MODE_COUNT, 2 * channel_count)
    scale = 1.0 / math.sqrt(ATOM_COUNT * MODE_COUNT)

    def per_block(inputs):
        which, offsets_block, kinds, listed, keep_mask = inputs
        lateral_block = which // transverse_span
        transverse_block = which % transverse_span
        angles = phase_table(wavevectors, lateral_block, transverse_block, offsets_block, lateral_span, transverse_span)
        distant = jnp.dot(jnp.cos(angles), filtered[:, :channel_count], precision=HIGHEST, preferred_element_type=jnp.float32)
        distant = distant + jnp.dot(jnp.sin(angles), filtered[:, channel_count:], precision=HIGHEST, preferred_element_type=jnp.float32)
        distant = distant * scale
        source_block = listed // ATOM_DEV
        lateral_shift = jnp.remainder(source_block // transverse_span - lateral_block + 1, lateral_span) - 1
        transverse_shift = jnp.remainder(source_block % transverse_span - transverse_block + 1, transverse_span) - 1
        own_embed = species_embed[kinds]
        nearby = edge_messages(values[listed], positions[listed], jnp.transpose(offsets_block), lateral_shift, transverse_shift, keep_mask, own_embed, atom_embed[listed], radial_weight, mixing_weight)
        return nearby + distant
    updated = lax.map(per_block, (block_index, block_offsets, block_species, block_neighbours, block_masks))
    return updated.reshape(lateral_span, transverse_span, ATOM_DEV, channel_count)
```

```python
import math

import jax
import jax.numpy as jnp
from jax import lax
from jax.experimental import pallas as pl
from jax.experimental.pallas import tpu as pltpu
from jax.sharding import PartitionSpec as P

MESH = pl.DeviceIdType.MESH
F32 = jnp.float32
BF16 = jnp.bfloat16

GX = 32
GY = 16
NZ = 16
ATOMS = 128
CH = 256
MODES = 512
SLOTS = 8
RADIAL = 64
SCALE = 1.0 / math.sqrt(33554432)
TURN = 2.0 * math.pi

COS_TERMS = [(-1.0) ** n * TURN ** (2 * n) / math.factorial(2 * n) for n in range(7)]
SIN_TERMS = [(-1.0) ** n * TURN ** (2 * n + 1) / math.factorial(2 * n + 1) for n in range(7)]


def halves(x):
    hi = x.astype(BF16)
    return hi, (x - hi.astype(F32)).astype(BF16)


def mm(a, b):
    return jnp.dot(a, b, preferred_element_type=F32)


def mm3(a_hi, a_lo, b_hi, b_lo):
    return mm(a_hi, b_hi) + (mm(a_hi, b_lo) + mm(a_lo, b_hi))


def cos_sin(turns):
    q = jnp.floor(turns * 2.0 + 0.5)
    r = turns - q * 0.5
    h = q * 0.5
    sign = 1.0 - 4.0 * (h - jnp.floor(h))
    y = r * r
    c = jnp.full_like(y, COS_TERMS[6])
    s = jnp.full_like(y, SIN_TERMS[6])
    for n in range(5, -1, -1):
        c = c * y + COS_TERMS[n]
        s = s * y + SIN_TERMS[n]
    return c * sign, s * (r * sign)


def remote(src, dst, send, recv, gx, gy):
    return pltpu.make_async_remote_copy(
        src_ref=src, dst_ref=dst, send_sem=send, recv_sem=recv, device_id=(gx, gy), device_id_type=MESH
    )


def kernel(
    feat, offs, spec, neigh, mask, wv, wv_s, vw, radw, emb, mixw, gf,
    out,
    feat2, carry2, halo, tf, t_hi, t_lo, tt_hi, tt_lo, ncol, wpad,
    part, got1, sums, got2, rows16, filt1, filt2, filt3, rh_hi, rh_lo, lpeer, lgot,
    nb_pad, dist, spj, rowid, onehot, bh, bl, filt, wcat, mix_hi, mix_lo, vb,
    s_feat, r_feat, s_halo, r_halo, s_rs1, r_rs1, s_rs2, r_rs2, s_ag1, r_ag1, s_ag2, r_ag2, s_fin, r_fin,
):
    gx = lax.axis_index("gx")
    gy = lax.axis_index("gy")
    c = lax.rem(gx, 2)
    z = gx // 2
    px = gy // 4
    py = lax.rem(gy, 4)
    peer = gx + 1 - 2 * c
    other = lax.rem(gx + 31 + 2 * c, GX)

    def plane(k):
        return lax.rem(px + k // 4, 4) * 4 + lax.rem(py + k % 4, 4)

    def column(k):
        return 2 * lax.rem(z + k, NZ) + c

    barrier = pltpu.get_barrier_semaphore()
    greeted = [(gx, plane(k)) for k in range(1, 16)]
    greeted += [(column(k), gy) for k in range(1, 16)]
    greeted += [(peer, gy), (other, gy)]
    up = lax.rem(gy + 1, GY)
    down = lax.rem(gy + GY - 1, GY)
    for device in greeted:
        pl.semaphore_signal(barrier, inc=1, device_id=device, device_id_type=MESH)

    f_hi, f_lo = halves(feat[0, 0])
    vw_hi, vw_lo = halves(vw[...])
    halo[4, 0:CH, :] = jnp.transpose(mm3(f_hi, f_lo, vw_hi, vw_lo))
    halo[4, CH:CH + 8, :] = jnp.zeros((8, ATOMS), F32)
    halo[4, CH:CH + 3, :] = offs[0, 0]
    halo[4, CH + 3:CH + 4, :] = spec[0].astype(F32)

    wpad[...] = jnp.zeros(wpad.shape, F32)
    wpad[0:3, :] = wv[...].astype(F32)
    r = lax.broadcasted_iota(jnp.int32, (256, MODES), 0)
    m = lax.broadcasted_iota(jnp.int32, (256, MODES), 1)
    pick = jnp.where((2 * (r & 15) + c) * 16 + (r >> 4) == m, 1.0, 0.0).astype(BF16)
    ncol[...] = lax.dot_general(
        pick, wpad[...].astype(BF16), (((1,), (1,)), ((), ())), preferred_element_type=F32
    )

    pl.semaphore_wait(barrier, len(greeted))

    sends = []

    def start(*a):
        copy = remote(*a)
        copy.start()
        sends.append(copy)

    def arrived(dst, sem):
        remote(dst, dst, s_fin.at[0], sem, peer, gy).wait_recv()

    start(halo.at[4, pl.ds(CH, 8)], carry2, s_feat.at[0], r_feat.at[0], peer, gy)
    start(feat.at[0, 0], feat2, s_feat.at[1], r_feat.at[1], peer, gy)
    start(halo.at[4], halo.at[3], s_halo.at[0], r_halo.at[0], gx, up)
    start(halo.at[4], halo.at[5], s_halo.at[1], r_halo.at[1], gx, down)
    start(halo.at[4], halo.at[(2 - 2 * c) * 3 + 1], s_halo.at[6], r_halo.at[6], other, gy)
    start(halo.at[4], halo.at[2 * c * 3 + 1], s_halo.at[3], r_halo.at[3], peer, gy)

    def table(block, positions, lane):
        def step(i, carry):
            n = ncol[pl.ds(pl.multiple_of(i * 64, 64), 64), :]
            n0, n1, n2 = n[:, 0:1], n[:, 1:2], n[:, 2:3]
            w0 = (n0.astype(jnp.int32) * block & 31).astype(F32)
            w1 = (n1.astype(jnp.int32) * gy & 15).astype(F32)
            turns = (w0 + n0 * positions[0:1, :]) * (1.0 / 32)
            turns = turns + (w1 + n1 * positions[1:2, :]) * (1.0 / 16)
            turns = turns + n2 * positions[2:3, :]
            cosine, sine = cos_sin(turns)
            for at, value in ((0, cosine), (64, sine)):
                tf[i, at:at + 64, lane:lane + ATOMS] = value
                hi, lo = halves(value)
                t_hi[i, at:at + 64, lane:lane + ATOMS] = hi
                t_lo[i, at:at + 64, lane:lane + ATOMS] = lo
            return carry

        lax.fori_loop(0, 4, step, 0)

    table(gx, halo[4, CH:CH + 8, :], 0)
    arrived(carry2, r_feat.at[0])
    table(peer, carry2[...], ATOMS)
    arrived(feat2, r_feat.at[1])
    g_hi, g_lo = halves(feat2[...])
    both_hi = jnp.concatenate([f_hi, g_hi], axis=0)
    both_lo = jnp.concatenate([f_lo, g_lo], axis=0)
    for dx in (2, 1, 3, 0):
        xx = lax.rem(px + dx, 4)
        a_hi, a_lo = t_hi[xx], t_lo[xx]
        p = mm3(a_hi, a_lo, both_hi, both_lo)
        for y in range(4):
            part[xx * 4 + y, :, 0:CH] = p[16 * y:16 * y + 16]
            part[xx * 4 + y, :, CH:2 * CH] = p[64 + 16 * y:64 + 16 * y + 16]
        for dy in (2, 1, 3, 0):
            k = dx * 4 + dy
            if k:
                start(part.at[plane(k)], got1.at[k], s_rs1.at[k], r_rs1.at[k], gx, plane(k))

    for t, slot in ((0, 3), (2, 5)):
        arrived(halo.at[slot], r_halo.at[t // 2])
        start(halo.at[slot], halo.at[(2 - 2 * c) * 3 + t], s_halo.at[5 + t], r_halo.at[5 + t], other, gy)
        start(halo.at[slot], halo.at[2 * c * 3 + t], s_halo.at[2 + t], r_halo.at[2 + t], peer, gy)

    for i in range(4):
        hi, lo = halves(jnp.transpose(tf[i]))
        tt_hi[:, 128 * i:128 * i + 128] = hi
        tt_lo[:, 128 * i:128 * i + 128] = lo
    wt = jnp.transpose(jnp.concatenate([radw[...], emb[...]], axis=0))
    hi, lo = halves(wt)
    wcat[:, 0:128] = hi
    wcat[:, 128:256] = lo
    hi, lo = halves(jnp.transpose(mixw[...]))
    mix_hi[...] = hi
    mix_lo[...] = lo
    nb_pad[...] = jnp.zeros(nb_pad.shape, jnp.int32)
    nb_pad[:, 0:SLOTS] = jnp.where(mask[0, 0] > 0, neigh[0, 0], -1)
    listed = jnp.transpose(nb_pad[...])[0:SLOTS]

    for t in range(3):
        arrived(halo.at[(2 - 2 * c) * 3 + t], r_halo.at[2 + t])
        arrived(halo.at[2 * c * 3 + t], r_halo.at[5 + t])

    source = listed >> 7
    atom = listed & 127
    s = (((source >> 4) - gx + 1) & 31) - 1
    t = (((source & 15) - gy + 1) & 15) - 1
    near = (s + 1) * 3 + (t + 1)
    found = [jnp.zeros((SLOTS, ATOMS), F32) for _ in range(4)]
    for j in range(9):
        for i in range(4):
            row = jnp.broadcast_to(halo[j, CH + i:CH + i + 1, :], (SLOTS, ATOMS))
            taken = jnp.take_along_axis(row, atom, axis=1)
            found[i] = jnp.where(near == j, taken, found[i])
    own = halo[4, CH:CH + 8, :]
    gap0 = (s.astype(F32) + found[0]) - own[0:1, :]
    gap1 = (t.astype(F32) + found[1]) - own[1:2, :]
    gap2 = found[2] - own[2:3, :]
    dist[...] = jnp.sqrt(gap0 * gap0 + gap1 * gap1 + gap2 * gap2 + 0.01)
    spj[...] = found[3]
    rowid[...] = jnp.where(listed < 0, -1, near * ATOMS + atom)
    own_kind = own[3:4, :]

    def slot_step(e, carry):
        lanes = pl.ds(pl.multiple_of(e * ATOMS, ATOMS), ATOMS)
        k = lax.broadcasted_iota(jnp.int32, (RADIAL, ATOMS), 0).astype(F32)
        scaled = (dist[pl.ds(e, 1), :] - k * (3.0 / 63)) / (6.0 / 63)
        hi, lo = halves(jnp.exp(-scaled * scaled))
        kinds = jnp.where(k == spj[pl.ds(e, 1), :], 1.0, 0.0) + jnp.where(k == own_kind, 1.0, 0.0)
        kinds = kinds.astype(BF16)
        bh[0:64, lanes] = hi
        bh[64:128, lanes] = kinds
        bh[128:192, lanes] = hi
        bh[192:256, lanes] = kinds
        bl[:, lanes] = lo
        place = rowid[pl.ds(e, 1), :]
        at = lax.broadcasted_iota(jnp.int32, (ATOMS, ATOMS), 0)
        for j in range(9):
            hit = jnp.where(at == place - ATOMS * j, 1.0, 0.0)
            onehot[ATOMS * j:ATOMS * j + ATOMS, lanes] = hit.astype(BF16)
        return carry

    lax.fori_loop(0, SLOTS, slot_step, 0)

    def filter_step(e, carry):
        lanes = pl.ds(pl.multiple_of(e * 256, 256), 256)
        before = mm(wcat[...], bh[:, lanes]) + mm(wcat[:, 0:64], bl[:, lanes])
        hi, lo = halves(before / (1.0 + jnp.exp(-before)))
        filt[:, lanes] = mm3(mix_hi[...], mix_lo[...], hi, lo)
        return carry

    lax.fori_loop(0, 4, filter_step, 0)

    total = part[gy]
    for k in range(1, 16):
        arrived(got1.at[k], r_rs1.at[k])
        total = total + got1[k]
    for k in range(NZ):
        sums[k] = total[k:k + 1, :]
    for k in range(1, 16):
        dz = lax.rem(z + k, NZ)
        start(sums.at[dz], got2.at[k], s_rs2.at[k], r_rs2.at[k], 2 * dz + c, gy)

    gf_hi, gf_lo = halves(gf[0])
    mode = gx * 16 + gy
    wave0 = jnp.full((1, CH), wv_s[0, mode], jnp.int32).astype(F32) * (TURN / 32)
    wave1 = jnp.full((1, CH), wv_s[1, mode], jnp.int32).astype(F32) * (TURN / 16)
    wave2 = jnp.full((1, CH), wv_s[2, mode], jnp.int32).astype(F32) * TURN
    damp = jnp.exp(-0.01 * (wave0 * wave0 + wave1 * wave1 + wave2 * wave2)) * SCALE
    rows16[...] = jnp.zeros(rows16.shape, F32)

    total = sums[z]
    for k in range(1, 16):
        arrived(got2.at[k], r_rs2.at[k])
        total = total + got2[k]
    rows16[0:1, :] = total[:, 0:CH]
    rows16[1:2, :] = total[:, CH:2 * CH]
    a_hi, a_lo = halves(rows16[...])
    mixed = mm3(a_hi, a_lo, gf_hi, gf_lo)
    filt1[z, :, 0:CH] = mixed[0:1, :] * damp
    filt1[z, :, CH:2 * CH] = mixed[1:2, :] * damp
    for k in range(1, 16):
        dz = lax.rem(z + k, NZ)
        start(filt1.at[z], filt1.at[z], s_ag1.at[k], r_ag1.at[k], 2 * dz + c, gy)
    for k in range(1, 16):
        arrived(filt1.at[lax.rem(z + NZ - k, NZ)], r_ag1.at[k])
    for k in range(NZ):
        filt2[k:k + 1, :] = filt1[k]
    for k in (10, 9, 11, 6, 14, 8, 2, 5, 7, 13, 15, 4, 12, 1, 3):
        start(filt2, filt3.at[gy], s_ag2.at[k], r_ag2.at[k], gx, plane(k))
    filt3[gy] = filt2[...]

    for j in range(9):
        hi, lo = halves(halo[j, 0:CH, :])
        vb[0:CH, ATOMS * j:ATOMS * j + ATOMS] = hi
        vb[CH:2 * CH, ATOMS * j:ATOMS * j + ATOMS] = lo

    def gather_step(e, acc):
        lanes = pl.ds(pl.multiple_of(e * 256, 256), 256)
        g = mm(vb[...], onehot[:, lanes])
        msg = (g[0:CH] + g[CH:2 * CH]) * filt[:, lanes]
        return acc + (msg[:, 0:ATOMS] + msg[:, ATOMS:2 * ATOMS])

    short = lax.fori_loop(0, 4, gather_step, jnp.zeros((CH, ATOMS), F32))
    out[0, 0] = jnp.transpose(short) * (1.0 / math.sqrt(SLOTS))

    for k in range(1, 16):
        arrived(filt3.at[lax.rem(px + 4 - k // 4, 4) * 4 + lax.rem(py + 4 - k % 4, 4)], r_ag2.at[k])
    for i in range(4):
        for y in range(4):
            hi, lo = halves(filt3[4 * i + y])
            for at, lane in ((0, 0), (64, CH)):
                row = 128 * i + at + 16 * y
                rh_hi[row:row + 16, :] = hi[:, lane:lane + CH]
                rh_lo[row:row + 16, :] = lo[:, lane:lane + CH]
    lpeer[...] = mm3(tt_hi[ATOMS:], tt_lo[ATOMS:], rh_hi[...], rh_lo[...])
    start(lpeer, lgot, s_fin.at[0], r_fin.at[0], peer, gy)
    mine = mm3(tt_hi[0:ATOMS], tt_lo[0:ATOMS], rh_hi[...], rh_lo[...])
    base = out[0, 0] + mine
    arrived(lgot, r_fin.at[0])
    out[0, 0] = base + lgot[...]
    for copy in sends:
        copy.wait_send()


def shards(features, offsets, species, neighbours, edge_mask, wavevectors, vw, radw, emb, mixw, gf):
    vmem = pl.BlockSpec(memory_space=pltpu.VMEM)
    smem = pl.BlockSpec(memory_space=pltpu.SMEM)
    dma = pltpu.SemaphoreType.DMA
    scratch = [
        pltpu.VMEM((ATOMS, CH), F32),
        pltpu.VMEM((8, ATOMS), F32),
        pltpu.VMEM((9, CH + 8, ATOMS), F32),
        pltpu.VMEM((4, 128, 2 * ATOMS), F32),
        pltpu.VMEM((4, 128, 2 * ATOMS), BF16),
        pltpu.VMEM((4, 128, 2 * ATOMS), BF16),
        pltpu.VMEM((2 * ATOMS, 512), BF16),
        pltpu.VMEM((2 * ATOMS, 512), BF16),
        pltpu.VMEM((256, 128), F32),
        pltpu.VMEM((128, MODES), F32),
        pltpu.VMEM((GY, NZ, 2 * CH), F32),
        pltpu.VMEM((GY, NZ, 2 * CH), F32),
        pltpu.VMEM((NZ, 1, 2 * CH), F32),
        pltpu.VMEM((NZ, 1, 2 * CH), F32),
        pltpu.VMEM((16, CH), F32),
        pltpu.VMEM((NZ, 1, 2 * CH), F32),
        pltpu.VMEM((NZ, 2 * CH), F32),
        pltpu.VMEM((GY, NZ, 2 * CH), F32),
        pltpu.VMEM((512, CH), BF16),
        pltpu.VMEM((512, CH), BF16),
        pltpu.VMEM((ATOMS, CH), F32),
        pltpu.VMEM((ATOMS, CH), F32),
        pltpu.VMEM((ATOMS, ATOMS), jnp.int32),
        pltpu.VMEM((SLOTS, ATOMS), F32),
        pltpu.VMEM((SLOTS, ATOMS), F32),
        pltpu.VMEM((SLOTS, ATOMS), jnp.int32),
        pltpu.VMEM((9 * ATOMS, SLOTS * ATOMS), BF16),
        pltpu.VMEM((256, SLOTS * ATOMS), BF16),
        pltpu.VMEM((64, SLOTS * ATOMS), BF16),
        pltpu.VMEM((CH, SLOTS * ATOMS), F32),
        pltpu.VMEM((CH, 256), BF16),
        pltpu.VMEM((CH, CH), BF16),
        pltpu.VMEM((CH, CH), BF16),
        pltpu.VMEM((2 * CH, 9 * ATOMS), BF16),
        dma((2,)), dma((2,)),
        dma((8,)), dma((8,)),
        dma((16,)), dma((16,)),
        dma((16,)), dma((16,)),
        dma((16,)), dma((16,)),
        dma((16,)), dma((16,)),
        dma((1,)), dma((1,)),
    ]
    return pl.pallas_call(
        kernel,
        out_shape=jax.ShapeDtypeStruct((1, 1, ATOMS, CH), F32),
        in_specs=[vmem] * 6 + [smem] + [vmem] * 5,
        out_specs=vmem,
        scratch_shapes=scratch,
        compiler_params=pltpu.CompilerParams(
            collective_id=0, has_side_effects=True, vmem_limit_bytes=40 * 1024 * 1024
        ),
    )(features, offsets, species, neighbours, edge_mask, wavevectors, wavevectors, vw, radw, emb, mixw, gf)


def solution(mesh):
    block = P("gx", "gy", None, None)
    placed = (block, block, P("gx", "gy", None), block, block, P(), P(), P(), P(), P(), P("gx", None, None))
    return jax.shard_map(shards, mesh=mesh, in_specs=placed, out_specs=block, check_vma=False)
```

```python
import math

import jax
import jax.numpy as jnp
from jax import lax
from jax.experimental import pallas as pl
from jax.experimental.pallas import tpu as pltpu
from jax.sharding import PartitionSpec as P

MESH = pl.DeviceIdType.MESH
F32 = jnp.float32
BF16 = jnp.bfloat16

GX = 32
GY = 16
NZ = 16
ATOMS = 128
CH = 256
MODES = 512
SLOTS = 8
RADIAL = 64
SCALE = 1.0 / math.sqrt(33554432)
TURN = 2.0 * math.pi

PLANE_ORDER = (10, 9, 11, 6, 14, 8, 2, 5, 7, 13, 15, 4, 12, 1, 3)

COS_TERMS = [(-1.0) ** n * TURN ** (2 * n) / math.factorial(2 * n) for n in range(7)]
SIN_TERMS = [(-1.0) ** n * TURN ** (2 * n + 1) / math.factorial(2 * n + 1) for n in range(7)]


def halves(x):
    hi = x.astype(BF16)
    return hi, (x - hi.astype(F32)).astype(BF16)


def mm(a, b):
    return jnp.dot(a, b, preferred_element_type=F32)


def mm3(a_hi, a_lo, b_hi, b_lo):
    return mm(a_hi, b_hi) + (mm(a_hi, b_lo) + mm(a_lo, b_hi))


def cos_sin(turns):
    q = jnp.floor(turns * 2.0 + 0.5)
    r = turns - q * 0.5
    h = q * 0.5
    sign = 1.0 - 4.0 * (h - jnp.floor(h))
    y = r * r
    c = jnp.full_like(y, COS_TERMS[6])
    s = jnp.full_like(y, SIN_TERMS[6])
    for n in range(5, -1, -1):
        c = c * y + COS_TERMS[n]
        s = s * y + SIN_TERMS[n]
    return c * sign, s * (r * sign)


def remote(src, dst, send, recv, gx, gy):
    return pltpu.make_async_remote_copy(
        src_ref=src, dst_ref=dst, send_sem=send, recv_sem=recv, device_id=(gx, gy), device_id_type=MESH
    )


def kernel(
    feat_h, offs_h, spec_h, neigh_h, mask_h, wv_h, vw_h, radw_h, emb_h, mixw_h, gf_h,
    out,
    feat, offs, spec, neigh, mask, wv, vw, embed, mixw, gf,
    carry2, halo, tf, tt_hi, tt_lo, ncol, wpad,
    part, theirs, got0, got1, sums, got2, rows16, filt1, filt2, filt3, rh_hi, rh_lo, lsum, lpeer, lgot,
    dist, spj, rowid, onehot, bh, bl, filt, wcat, mix_hi, mix_lo, vb,
    ready, s_in, s_pair, r_pair, s_halo, r_halo, s_rs1, r_rs1, s_rs2, r_rs2, s_ag1, r_ag1, s_ag2, r_ag2,
):
    gx = lax.axis_index("gx")
    gy = lax.axis_index("gy")
    c = lax.rem(gx, 2)
    z = gx // 2
    px = gy // 4
    py = lax.rem(gy, 4)
    peer = gx + 1 - 2 * c
    other = lax.rem(gx + 31 + 2 * c, GX)
    up = lax.rem(gy + 1, GY)
    down = lax.rem(gy + GY - 1, GY)

    def plane(k):
        return lax.rem(px + k // 4, 4) * 4 + lax.rem(py + k % 4, 4)

    def column(k):
        return 2 * lax.rem(z + k, NZ) + c

    barrier = pltpu.get_barrier_semaphore()
    greeted = [(column(k), gy) for k in (4, 12, 3, 13, 2, 14, 1, 15)]
    greeted += [(gx, plane(k)) for k in PLANE_ORDER]
    greeted += [(other, gy), (peer, gy)]
    for device in greeted:
        pl.semaphore_signal(barrier, inc=1, device_id=device, device_id_type=MESH)

    loads = [
        pltpu.make_async_copy(src, dst, s_in.at[i])
        for i, (src, dst) in enumerate((
            (wv_h, wv), (offs_h.at[0], offs), (feat_h.at[0, 0], feat), (spec_h, spec), (vw_h, vw),
            (neigh_h.at[0, 0], neigh), (mask_h.at[0, 0], mask), (radw_h, embed.at[pl.ds(0, RADIAL)]),
            (emb_h, embed.at[pl.ds(RADIAL, RADIAL)]), (mixw_h, mixw), (gf_h.at[0], gf),
        ))
    ]
    for load in loads:
        load.start()
    for load in loads[0:3]:
        load.wait()

    wpad[...] = jnp.zeros(wpad.shape, F32)
    vectors = wv[...].astype(F32)
    wpad[0:3, :] = vectors
    r = lax.broadcasted_iota(jnp.int32, (MODES, MODES), 0)
    m = lax.broadcasted_iota(jnp.int32, (MODES, MODES), 1)
    group = 2 * ((z + 4 + 8 * ((r >> 7) & 1) + (r & 7)) & 15) + (c ^ (r >> 8))
    pick = jnp.where(group * 16 + ((r >> 3) & 15) == m, 1.0, 0.0).astype(BF16)
    ncol[...] = lax.dot_general(
        pick, wpad[...].astype(BF16), (((1,), (1,)), ((), ())), preferred_element_type=F32
    )

    def table(i, block, positions):
        n = ncol[pl.ds(pl.multiple_of(i * 64, 64), 64), :]
        n0, n1, n2 = n[:, 0:1], n[:, 1:2], n[:, 2:3]
        w0 = (n0.astype(jnp.int32) * block & 31).astype(F32)
        w1 = (n1.astype(jnp.int32) * gy & 15).astype(F32)
        turns = (w0 + n0 * positions[0]) * (1.0 / 32)
        turns = turns + (w1 + n1 * positions[1]) * (1.0 / 16)
        turns = turns + n2 * positions[2]
        return jnp.concatenate(cos_sin(turns), axis=0)

    f_hi, f_lo = halves(feat[...])

    def own_table(i):
        both = table(i, gx, [offs[0], offs[1], offs[2]])
        t_hi, t_lo = halves(both)
        return both, mm3(t_hi, t_lo, f_hi, f_lo)

    def mine_step(i, carry):
        both, p = own_table(i)
        tf[i, :, 0:ATOMS] = both
        part[i, :, :, 0:CH] = p[0:64].reshape(8, 8, CH)
        part[i, :, :, CH:2 * CH] = p[64:128].reshape(8, 8, CH)
        return carry

    def theirs_step(i, carry):
        _, p = own_table(i + 4)
        theirs[i, :, :, 0:CH] = p[0:64].reshape(8, 8, CH)
        theirs[i, :, :, CH:2 * CH] = p[64:128].reshape(8, 8, CH)
        return carry

    lax.fori_loop(0, 4, theirs_step, 0)
    lax.fori_loop(0, 4, mine_step, 0)

    sends = []

    def start(src, dst, s_sems, r_sems, i, x, y):
        copy = remote(src, dst, s_sems.at[i], r_sems.at[i], x, y)
        copy.start()
        sends.append(copy)

    def arrived(dst, r_sems, i):
        remote(dst, dst, s_pair.at[0], r_sems.at[i], peer, gy).wait_recv()

    def drain():
        while sends:
            sends.pop().wait_send()

    pl.semaphore_wait(barrier, len(greeted))
    for k in (4, 12):
        pl.semaphore_signal(ready, inc=1, device_id=(column(k), gy), device_id_type=MESH)
    for q in range(2):
        start(theirs.at[pl.ds(2 * q, 2)], got0.at[pl.ds(2 * q, 2)], s_pair, r_pair, q, peer, gy)

    for q in range(2):
        arrived(got0.at[pl.ds(2 * q, 2)], r_pair, q)
        part[2 * q:2 * q + 2] = part[2 * q:2 * q + 2] + got0[2 * q:2 * q + 2]
        for k in PLANE_ORDER:
            to = plane(k)
            start(part.at[2 * q + to // 8, lax.rem(to, 8)], got1.at[q, k], s_rs1, r_rs1, 16 * q + k, gx, to)

    for load in loads[3:5]:
        load.wait()
    vw_hi, vw_lo = halves(vw[...])
    halo[4, 0:CH, :] = jnp.transpose(mm3(f_hi, f_lo, vw_hi, vw_lo))
    halo[4, CH:CH + 8, :] = jnp.zeros((8, ATOMS), F32)
    for i in range(3):
        halo[4, CH + i:CH + i + 1, :] = offs[i]
    halo[4, CH + 3:CH + 4, :] = spec[0].astype(F32)
    start(halo.at[4, pl.ds(CH, 8)], carry2, s_pair, r_pair, 2, peer, gy)
    start(halo.at[4], halo.at[7 - 6 * c], s_halo, r_halo, 1, other, gy)
    start(halo.at[4], halo.at[1 + 6 * c], s_halo, r_halo, 0, peer, gy)
    pl.semaphore_wait(ready, 2)

    for q in range(2):
        total = part[2 * q + gy // 8, lax.rem(gy, 8)]
        for k in range(1, 16):
            arrived(got1.at[q, k], r_rs1, 16 * q + k)
            total = total + got1[q, k]
        for k in range(8):
            sums[8 * q + k] = total[k:k + 1, :]
        for k in (4, 3, 5, 2, 6, 1, 7, 0):
            d = (4 + 8 * q + k) % 16
            if d:
                start(sums.at[8 * q + k], got2.at[d], s_rs2, r_rs2, d, column(d), gy)

    arrived(halo.at[7 - 6 * c], r_halo, 0)
    arrived(halo.at[1 + 6 * c], r_halo, 1)
    for i in range(3):
        start(halo.at[3 * i + 1], halo.at[3 * i], s_halo, r_halo, 2 + i, gx, up)
        start(halo.at[3 * i + 1], halo.at[3 * i + 2], s_halo, r_halo, 5 + i, gx, down)

    for load in loads[5:]:
        load.wait()
    mine = lax.broadcasted_iota(jnp.int32, (3, MODES), 1) == gx * 16 + gy
    wave = jnp.sum(jnp.where(mine, vectors, 0.0), axis=1, keepdims=True)
    wave0 = wave[0:1] * (TURN / 32)
    wave1 = wave[1:2] * (TURN / 16)
    wave2 = wave[2:3] * TURN
    damp = jnp.exp(-0.01 * (wave0 * wave0 + wave1 * wave1 + wave2 * wave2)) * SCALE
    gf_hi, gf_lo = halves(gf[...])
    rows16[...] = jnp.zeros(rows16.shape, F32)

    arrived(carry2, r_pair, 2)

    def peer_step(i, carry):
        tf[i, :, ATOMS:2 * ATOMS] = table(i, peer, [carry2[0:1], carry2[1:2], carry2[2:3]])
        return carry

    lax.fori_loop(0, 4, peer_step, 0)
    for i in range(4):
        hi, lo = halves(jnp.transpose(tf[i]))
        tt_hi[i // 2, :, 128 * (i % 2):128 * (i % 2) + 128] = hi
        tt_lo[i // 2, :, 128 * (i % 2):128 * (i % 2) + 128] = lo
    wt = jnp.transpose(embed[...])
    hi, lo = halves(wt)
    wcat[:, 0:128] = hi
    wcat[:, 128:256] = lo
    hi, lo = halves(jnp.transpose(mixw[...]))
    mix_hi[...] = hi
    mix_lo[...] = lo

    listed = jnp.where(mask[...] > 0, neigh[...], -1)
    source = listed >> 7
    atom = listed & 127
    s = (((source >> 4) - gx + 1) & 31) - 1
    t = (((source & 15) - gy + 1) & 15) - 1
    near = (s + 1) * 3 + (t + 1)
    rowid[...] = jnp.where(listed < 0, -1, near * ATOMS + atom)

    def onehot_step(e, carry):
        lanes = pl.ds(pl.multiple_of(e * ATOMS, ATOMS), ATOMS)
        place = rowid[pl.ds(e, 1), :]
        at = lax.broadcasted_iota(jnp.int32, (ATOMS, ATOMS), 0)
        for j in range(9):
            hit = jnp.where(at == place - ATOMS * j, 1.0, 0.0)
            onehot[ATOMS * j:ATOMS * j + ATOMS, lanes] = hit.astype(BF16)
        return carry

    lax.fori_loop(0, SLOTS, onehot_step, 0)

    total = sums[12]
    for k in (1, 15, 2, 14, 3, 13, 4, 12, 5, 11, 6, 10, 7, 9, 8):
        arrived(got2.at[k], r_rs2, k)
        total = total + got2[k]
    rows16[0:1, :] = total[:, 0:CH]
    rows16[1:2, :] = total[:, CH:2 * CH]
    a_hi, a_lo = halves(rows16[...])
    mixed = mm3(a_hi, a_lo, gf_hi, gf_lo)
    filt1[12, :, 0:CH] = mixed[0:1, :] * damp
    filt1[12, :, CH:2 * CH] = mixed[1:2, :] * damp
    for d in (8, 7, 9, 6, 10, 5, 11, 4, 12, 3, 13, 2, 14, 1, 15):
        at = (12 - d) % 16
        start(filt1.at[12], filt1.at[at], s_ag1, r_ag1, at, column(d), gy)

    for i in range(3):
        arrived(halo.at[3 * i], r_halo, 2 + i)
        arrived(halo.at[3 * i + 2], r_halo, 5 + i)
    found = [jnp.zeros((SLOTS, ATOMS), F32) for _ in range(4)]
    for j in range(9):
        for i in range(4):
            row = jnp.broadcast_to(halo[j, CH + i:CH + i + 1, :], (SLOTS, ATOMS))
            taken = jnp.take_along_axis(row, atom, axis=1)
            found[i] = jnp.where(near == j, taken, found[i])
    own = halo[4, CH:CH + 8, :]
    gap0 = (s.astype(F32) + found[0]) - own[0:1, :]
    gap1 = (t.astype(F32) + found[1]) - own[1:2, :]
    gap2 = found[2] - own[2:3, :]
    dist[...] = jnp.sqrt(gap0 * gap0 + gap1 * gap1 + gap2 * gap2 + 0.01)
    spj[...] = found[3]
    own_kind = own[3:4, :]

    def basis_step(e, carry):
        lanes = pl.ds(pl.multiple_of(e * ATOMS, ATOMS), ATOMS)
        k = lax.broadcasted_iota(jnp.int32, (RADIAL, ATOMS), 0).astype(F32)
        scaled = (dist[pl.ds(e, 1), :] - k * (3.0 / 63)) / (6.0 / 63)
        hi, lo = halves(jnp.exp(-scaled * scaled))
        kinds = jnp.where(k == spj[pl.ds(e, 1), :], 1.0, 0.0) + jnp.where(k == own_kind, 1.0, 0.0)
        kinds = kinds.astype(BF16)
        bh[0:64, lanes] = hi
        bh[64:128, lanes] = kinds
        bh[128:192, lanes] = hi
        bh[192:256, lanes] = kinds
        bl[:, lanes] = lo
        return carry

    lax.fori_loop(0, SLOTS, basis_step, 0)

    def filter_step(e, carry):
        lanes = pl.ds(pl.multiple_of(e * 256, 256), 256)
        before = mm(wcat[...], bh[:, lanes]) + mm(wcat[:, 0:64], bl[:, lanes])
        hi, lo = halves(before / (1.0 + jnp.exp(-before)))
        filt[:, lanes] = mm3(mix_hi[...], mix_lo[...], hi, lo)
        return carry

    lax.fori_loop(0, 4, filter_step, 0)
    drain()

    def spread(q):
        for k in range(8):
            at = 8 * q + k
            if at != 12:
                arrived(filt1.at[at], r_ag1, at)
            filt2[q, k:k + 1, :] = filt1[at]
        for k in PLANE_ORDER:
            start(filt2.at[q], filt3.at[q, gy], s_ag2, r_ag2, 16 * q + k, gx, plane(k))
        filt3[q, gy] = filt2[q]

    spread(1)
    spread(0)

    for j in range(9):
        hi, lo = halves(halo[j, 0:CH, :])
        vb[0:CH, ATOMS * j:ATOMS * j + ATOMS] = hi
        vb[CH:2 * CH, ATOMS * j:ATOMS * j + ATOMS] = lo

    def gather_step(e, acc):
        lanes = pl.ds(pl.multiple_of(e * 256, 256), 256)
        g = mm(vb[...], onehot[:, lanes])
        msg = (g[0:CH] + g[CH:2 * CH]) * filt[:, lanes]
        return acc + (msg[:, 0:ATOMS] + msg[:, ATOMS:2 * ATOMS])

    short = lax.fori_loop(0, 4, gather_step, jnp.zeros((CH, ATOMS), F32))
    out[0, 0] = jnp.transpose(short) * (1.0 / math.sqrt(SLOTS))

    def factors(q):
        for k in range(1, 16):
            sender = lax.rem(px + 4 - k // 4, 4) * 4 + lax.rem(py + 4 - k % 4, 4)
            arrived(filt3.at[q, sender], r_ag2, 16 * q + k)
        for h in range(2):
            hi, lo = halves(filt3[q, 8 * h:8 * h + 8].reshape(64, 2 * CH))
            for at, lane in ((128 * h, 0), (128 * h + 64, CH)):
                rh_hi[at:at + 64, :] = hi[:, lane:lane + CH]
                rh_lo[at:at + 64, :] = lo[:, lane:lane + CH]

    def terms(q, rows):
        return mm3(tt_hi[q, rows], tt_lo[q, rows], rh_hi[...], rh_lo[...])

    near_rows, far_rows = slice(0, ATOMS), slice(ATOMS, 2 * ATOMS)
    factors(1)
    lsum[...] = terms(1, far_rows)
    out[0, 0] += terms(1, near_rows)
    drain()
    factors(0)
    lpeer[...] = lsum[...] + terms(0, far_rows)
    start(lpeer, lgot, s_pair, r_pair, 3, peer, gy)
    base = out[0, 0] + terms(0, near_rows)
    arrived(lgot, r_pair, 3)
    out[0, 0] = base + lgot[...]
    drain()


def shards(features, offsets, species, neighbours, edge_mask, wavevectors, vw, radw, emb, mixw, gf):
    vmem = pl.BlockSpec(memory_space=pltpu.VMEM)
    hbm = pl.BlockSpec(memory_space=pltpu.HBM)
    dma = pltpu.SemaphoreType.DMA
    scratch = [
        pltpu.VMEM((ATOMS, CH), F32),
        pltpu.VMEM((3, 1, ATOMS), F32),
        pltpu.VMEM((1, 1, ATOMS), jnp.int32),
        pltpu.VMEM((SLOTS, ATOMS), jnp.int32),
        pltpu.VMEM((SLOTS, ATOMS), jnp.int32),
        pltpu.VMEM((3, MODES), jnp.int32),
        pltpu.VMEM((CH, CH), F32),
        pltpu.VMEM((2 * RADIAL, CH), F32),
        pltpu.VMEM((CH, CH), F32),
        pltpu.VMEM((CH, CH), F32),
        pltpu.VMEM((8, ATOMS), F32),
        pltpu.VMEM((9, CH + 8, ATOMS), F32),
        pltpu.VMEM((4, 128, 2 * ATOMS), F32),
        pltpu.VMEM((2, 2 * ATOMS, 256), BF16),
        pltpu.VMEM((2, 2 * ATOMS, 256), BF16),
        pltpu.VMEM((MODES, 128), F32),
        pltpu.VMEM((128, MODES), F32),
        pltpu.VMEM((4, 8, 8, 2 * CH), F32),
        pltpu.VMEM((4, 8, 8, 2 * CH), F32),
        pltpu.VMEM((4, 8, 8, 2 * CH), F32),
        pltpu.VMEM((2, GY, 8, 2 * CH), F32),
        pltpu.VMEM((NZ, 1, 2 * CH), F32),
        pltpu.VMEM((NZ, 1, 2 * CH), F32),
        pltpu.VMEM((16, CH), F32),
        pltpu.VMEM((NZ, 1, 2 * CH), F32),
        pltpu.VMEM((2, 8, 2 * CH), F32),
        pltpu.VMEM((2, GY, 8, 2 * CH), F32),
        pltpu.VMEM((256, CH), BF16),
        pltpu.VMEM((256, CH), BF16),
        pltpu.VMEM((ATOMS, CH), F32),
        pltpu.VMEM((ATOMS, CH), F32),
        pltpu.VMEM((ATOMS, CH), F32),
        pltpu.VMEM((SLOTS, ATOMS), F32),
        pltpu.VMEM((SLOTS, ATOMS), F32),
        pltpu.VMEM((SLOTS, ATOMS), jnp.int32),
        pltpu.VMEM((9 * ATOMS, SLOTS * ATOMS), BF16),
        pltpu.VMEM((256, SLOTS * ATOMS), BF16),
        pltpu.VMEM((64, SLOTS * ATOMS), BF16),
        pltpu.VMEM((CH, SLOTS * ATOMS), F32),
        pltpu.VMEM((CH, 256), BF16),
        pltpu.VMEM((CH, CH), BF16),
        pltpu.VMEM((CH, CH), BF16),
        pltpu.VMEM((2 * CH, 9 * ATOMS), BF16),
        pltpu.SemaphoreType.REGULAR,
        dma((11,)),
        dma((4,)), dma((4,)),
        dma((8,)), dma((8,)),
        dma((32,)), dma((32,)),
        dma((16,)), dma((16,)),
        dma((16,)), dma((16,)),
        dma((32,)), dma((32,)),
    ]
    return pl.pallas_call(
        kernel,
        out_shape=jax.ShapeDtypeStruct((1, 1, ATOMS, CH), F32),
        in_specs=[hbm] * 11,
        out_specs=vmem,
        scratch_shapes=scratch,
        compiler_params=pltpu.CompilerParams(
            collective_id=0, has_side_effects=True, vmem_limit_bytes=56 * 1024 * 1024
        ),
    )(
        features, jnp.transpose(offsets, (0, 2, 1, 3)), species, jnp.swapaxes(neighbours, 2, 3),
        jnp.swapaxes(edge_mask, 2, 3), wavevectors, vw, radw, emb, mixw, gf,
    )


def solution(mesh):
    block = P("gx", "gy", None, None)
    placed = (block, block, P("gx", "gy", None), block, block, P(), P(), P(), P(), P(), P("gx", None, None))
    return jax.shard_map(shards, mesh=mesh, in_specs=placed, out_specs=block, check_vma=False)
```

```python
import math

import jax
import jax.numpy as jnp
from jax import lax
from jax.experimental import pallas as pl
from jax.experimental.pallas import tpu as pltpu
from jax.sharding import PartitionSpec as P

MESH = pl.DeviceIdType.MESH
F32 = jnp.float32
BF16 = jnp.bfloat16

GX = 32
GY = 16
NZ = 16
ATOMS = 128
CH = 256
MODES = 512
SLOTS = 8
RADIAL = 64
SCALE = 1.0 / math.sqrt(33554432)
TURN = 2.0 * math.pi

PLANE_ORDER = (10, 9, 11, 6, 14, 8, 2, 5, 7, 13, 15, 4, 12, 1, 3)

COS_TERMS = [(-1.0) ** n * TURN ** (2 * n) / math.factorial(2 * n) for n in range(7)]
SIN_TERMS = [(-1.0) ** n * TURN ** (2 * n + 1) / math.factorial(2 * n + 1) for n in range(7)]


def halves(x):
    hi = x.astype(BF16)
    return hi, (x - hi.astype(F32)).astype(BF16)


def mm(a, b):
    return jnp.dot(a, b, preferred_element_type=F32)


def mm3(a_hi, a_lo, b_hi, b_lo):
    return mm(a_hi, b_hi) + (mm(a_hi, b_lo) + mm(a_lo, b_hi))


def cos_sin(turns):
    q = jnp.floor(turns * 2.0 + 0.5)
    r = turns - q * 0.5
    h = q * 0.5
    sign = 1.0 - 4.0 * (h - jnp.floor(h))
    y = r * r
    c = jnp.full_like(y, COS_TERMS[6])
    s = jnp.full_like(y, SIN_TERMS[6])
    for n in range(5, -1, -1):
        c = c * y + COS_TERMS[n]
        s = s * y + SIN_TERMS[n]
    return c * sign, s * (r * sign)


def remote(src, dst, send, recv, gx, gy):
    return pltpu.make_async_remote_copy(
        src_ref=src, dst_ref=dst, send_sem=send, recv_sem=recv, device_id=(gx, gy), device_id_type=MESH
    )


def kernel(
    feat_h, offs_h, spec_h, neigh_h, mask_h, wv_h, vw_h, radw_h, emb_h, mixw_h, gf_h,
    out,
    feat, offs, spec, neigh, mask, wv, vw, embed, mixw, gf,
    near_pos, halo, tf, tt_hi, tt_lo, ncol, wpad,
    part, theirs, got0, got1, sums, got2, rows16, filt1, filt2, filt3, rh_hi, rh_lo, lsum, lpeer, lgot,
    dist, spj, rowid, onehot, bh, bl, filt, wcat, mix_hi, mix_lo, vb,
    ready, s_in, s_pair, r_pair, s_pos, r_pos, s_halo, r_halo, s_rs1, r_rs1, s_rs2, r_rs2, s_ag1, r_ag1, s_ag2, r_ag2,
):
    gx = lax.axis_index("gx")
    gy = lax.axis_index("gy")
    c = lax.rem(gx, 2)
    z = gx // 2
    px = gy // 4
    py = lax.rem(gy, 4)
    peer = gx + 1 - 2 * c
    other = lax.rem(gx + 31 + 2 * c, GX)
    up = lax.rem(gy + 1, GY)
    down = lax.rem(gy + GY - 1, GY)

    def plane(k):
        return lax.rem(px + k // 4, 4) * 4 + lax.rem(py + k % 4, 4)

    def column(k):
        return 2 * lax.rem(z + k, NZ) + c

    to_peer, to_other = 3 * (2 * c), 3 * (2 - 2 * c)
    around = [
        (peer, gy, to_peer + 1), (peer, up, to_peer), (peer, down, to_peer + 2),
        (other, gy, to_other + 1), (other, up, to_other), (other, down, to_other + 2),
        (gx, up, 3), (gx, down, 5),
    ]
    from_peer, from_other = to_other, to_peer
    slots_here = [
        from_peer + 1, from_peer, from_peer + 2, from_other + 1, from_other, from_other + 2, 3, 5,
    ]

    barrier = pltpu.get_barrier_semaphore()
    greeted = [(column(k), gy) for k in (4, 12, 3, 13, 2, 14, 1, 15)]
    greeted += [(gx, plane(k)) for k in PLANE_ORDER]
    greeted += [(other, up), (other, down), (peer, up), (peer, down), (other, gy), (peer, gy)]
    for device in greeted:
        pl.semaphore_signal(barrier, inc=1, device_id=device, device_id_type=MESH)

    loads = [
        pltpu.make_async_copy(src, dst, s_in.at[i])
        for i, (src, dst) in enumerate((
            (wv_h, wv), (offs_h.at[0], offs), (feat_h.at[0, 0], feat), (spec_h, spec), (vw_h, vw),
            (neigh_h.at[0, 0], neigh), (mask_h.at[0, 0], mask), (radw_h, embed.at[pl.ds(0, RADIAL)]),
            (emb_h, embed.at[pl.ds(RADIAL, RADIAL)]), (mixw_h, mixw), (gf_h.at[0], gf),
        ))
    ]
    for load in loads:
        load.start()
    for load in loads[0:4]:
        load.wait()
    near_pos[4] = jnp.zeros((8, ATOMS), F32)
    for i in range(3):
        near_pos[4, i:i + 1, :] = offs[i]
    near_pos[4, 3:4, :] = spec[0].astype(F32)

    wpad[...] = jnp.zeros(wpad.shape, F32)
    vectors = wv[...].astype(F32)
    wpad[0:3, :] = vectors
    even = wpad[0:8, :]
    odd = pltpu.roll(even, MODES - 16, 1)
    wpad[0:8, :] = jnp.where(c == 0, even, odd)
    wpad[8:16, :] = jnp.where(c == 0, odd, even)
    r = lax.broadcasted_iota(jnp.int32, (256, 1), 0)
    m = lax.broadcasted_iota(jnp.int32, (256, MODES), 1)
    target = 32 * ((z + 4 + 8 * (r >> 7) + (r & 7)) & 15) + ((r >> 3) & 15)
    pick = jnp.where(m == target, 1.0, 0.0).astype(BF16)
    ncol[...] = lax.dot_general(
        pick, wpad[...].astype(BF16), (((1,), (1,)), ((), ())), preferred_element_type=F32
    )

    def table(i, parity, block, positions):
        n = ncol[pl.ds(pl.multiple_of(i * 64, 64), 64), :]
        n0, n1, n2 = [n[:, 8 * parity + a:8 * parity + a + 1] for a in range(3)]
        w0 = (n0.astype(jnp.int32) * block & 31).astype(F32)
        w1 = (n1.astype(jnp.int32) * gy & 15).astype(F32)
        turns = (w0 + n0 * positions[0]) * (1.0 / 32)
        turns = turns + (w1 + n1 * positions[1]) * (1.0 / 16)
        turns = turns + n2 * positions[2]
        return jnp.concatenate(cos_sin(turns), axis=0)

    f_hi, f_lo = halves(feat[...])

    def own_table(i, parity, into):
        both = table(i, parity, gx, [offs[0], offs[1], offs[2]])
        t_hi, t_lo = halves(both)
        p = mm3(t_hi, t_lo, f_hi, f_lo)
        into[i, :, :, 0:CH] = p[0:64].reshape(8, 8, CH)
        into[i, :, :, CH:2 * CH] = p[64:128].reshape(8, 8, CH)
        return both

    def own_step(i, carry):
        own_table(i, 1, theirs)
        tf[i, :, 0:ATOMS] = own_table(i, 0, part)
        return carry

    lax.fori_loop(0, 4, own_step, 0)

    sends = []

    def start(src, dst, s_sems, r_sems, i, x, y):
        copy = remote(src, dst, s_sems.at[i], r_sems.at[i], x, y)
        copy.start()
        sends.append(copy)

    def arrived(dst, r_sems, i):
        remote(dst, dst, s_pair.at[0], r_sems.at[i], peer, gy).wait_recv()

    def drain():
        while sends:
            sends.pop().wait_send()

    pl.semaphore_wait(barrier, len(greeted))
    for k in (4, 12):
        pl.semaphore_signal(ready, inc=1, device_id=(column(k), gy), device_id_type=MESH)
    for q in range(2):
        start(theirs.at[pl.ds(2 * q, 2)], got0.at[pl.ds(2 * q, 2)], s_pair, r_pair, q, peer, gy)

    for i, (x, y, slot) in enumerate(around):
        start(near_pos.at[4], near_pos.at[slot], s_pos, r_pos, i, x, y)

    for q in range(2):
        arrived(got0.at[pl.ds(2 * q, 2)], r_pair, q)
        part[2 * q:2 * q + 2] = part[2 * q:2 * q + 2] + got0[2 * q:2 * q + 2]
        for k in PLANE_ORDER:
            to = plane(k)
            start(part.at[2 * q + to // 8, lax.rem(to, 8)], got1.at[q, k], s_rs1, r_rs1, 16 * q + k, gx, to)

    loads[4].wait()
    vw_hi, vw_lo = halves(vw[...])
    halo[4] = jnp.transpose(mm3(f_hi, f_lo, vw_hi, vw_lo))
    start(halo.at[4], halo.at[7 - 6 * c], s_halo, r_halo, 1, other, gy)
    start(halo.at[4], halo.at[1 + 6 * c], s_halo, r_halo, 0, peer, gy)
    pl.semaphore_wait(ready, 2)

    for q in range(2):
        total = part[2 * q + gy // 8, lax.rem(gy, 8)]
        for k in range(1, 16):
            arrived(got1.at[q, k], r_rs1, 16 * q + k)
            total = total + got1[q, k]
        for k in range(8):
            sums[8 * q + k] = total[k:k + 1, :]
        for k in (4, 3, 5, 2, 6, 1, 7, 0):
            d = (4 + 8 * q + k) % 16
            if d:
                start(sums.at[8 * q + k], got2.at[d], s_rs2, r_rs2, d, column(d), gy)

    arrived(halo.at[7 - 6 * c], r_halo, 0)
    arrived(halo.at[1 + 6 * c], r_halo, 1)
    for i in range(3):
        start(halo.at[3 * i + 1], halo.at[3 * i], s_halo, r_halo, 2 + i, gx, up)
        start(halo.at[3 * i + 1], halo.at[3 * i + 2], s_halo, r_halo, 5 + i, gx, down)

    for load in loads[5:]:
        load.wait()
    mine = lax.broadcasted_iota(jnp.int32, (3, MODES), 1) == gx * 16 + gy
    wave = jnp.sum(jnp.where(mine, vectors, 0.0), axis=1, keepdims=True)
    wave0 = wave[0:1] * (TURN / 32)
    wave1 = wave[1:2] * (TURN / 16)
    wave2 = wave[2:3] * TURN
    damp = jnp.exp(-0.01 * (wave0 * wave0 + wave1 * wave1 + wave2 * wave2)) * SCALE
    gf_hi, gf_lo = halves(gf[...])
    rows16[...] = jnp.zeros(rows16.shape, F32)

    for i, slot in enumerate(slots_here):
        arrived(near_pos.at[slot], r_pos, i)

    def peer_step(i, carry):
        there = near_pos[from_peer + 1]
        tf[i, :, ATOMS:2 * ATOMS] = table(i, 0, peer, [there[0:1], there[1:2], there[2:3]])
        return carry

    lax.fori_loop(0, 4, peer_step, 0)
    for i in range(4):
        hi, lo = halves(jnp.transpose(tf[i]))
        tt_hi[i // 2, :, 128 * (i % 2):128 * (i % 2) + 128] = hi
        tt_lo[i // 2, :, 128 * (i % 2):128 * (i % 2) + 128] = lo
    wt = jnp.transpose(embed[...])
    hi, lo = halves(wt)
    wcat[:, 0:128] = hi
    wcat[:, 128:256] = lo
    hi, lo = halves(jnp.transpose(mixw[...]))
    mix_hi[...] = hi
    mix_lo[...] = lo

    listed = jnp.where(mask[...] > 0, neigh[...], -1)
    source = listed >> 7
    atom = listed & 127
    s = (((source >> 4) - gx + 1) & 31) - 1
    t = (((source & 15) - gy + 1) & 15) - 1
    near = (s + 1) * 3 + (t + 1)
    rowid[...] = jnp.where(listed < 0, -1, near * ATOMS + atom)

    def onehot_step(e, carry):
        lanes = pl.ds(pl.multiple_of(e * ATOMS, ATOMS), ATOMS)
        place = rowid[pl.ds(e, 1), :]
        at = lax.broadcasted_iota(jnp.int32, (ATOMS, ATOMS), 0)
        for j in range(9):
            hit = jnp.where(at == place - ATOMS * j, 1.0, 0.0)
            onehot[ATOMS * j:ATOMS * j + ATOMS, lanes] = hit.astype(BF16)
        return carry

    lax.fori_loop(0, SLOTS, onehot_step, 0)

    found = [jnp.zeros((SLOTS, ATOMS), F32) for _ in range(4)]
    for j in range(9):
        for i in range(4):
            row = jnp.broadcast_to(near_pos[j, i:i + 1, :], (SLOTS, ATOMS))
            taken = jnp.take_along_axis(row, atom, axis=1)
            found[i] = jnp.where(near == j, taken, found[i])
    own = near_pos[4]
    gap0 = (s.astype(F32) + found[0]) - own[0:1, :]
    gap1 = (t.astype(F32) + found[1]) - own[1:2, :]
    gap2 = found[2] - own[2:3, :]
    dist[...] = jnp.sqrt(gap0 * gap0 + gap1 * gap1 + gap2 * gap2 + 0.01)
    spj[...] = found[3]
    own_kind = own[3:4, :]

    def basis_step(e, carry):
        lanes = pl.ds(pl.multiple_of(e * ATOMS, ATOMS), ATOMS)
        k = lax.broadcasted_iota(jnp.int32, (RADIAL, ATOMS), 0).astype(F32)
        scaled = (dist[pl.ds(e, 1), :] - k * (3.0 / 63)) / (6.0 / 63)
        hi, lo = halves(jnp.exp(-scaled * scaled))
        kinds = jnp.where(k == spj[pl.ds(e, 1), :], 1.0, 0.0) + jnp.where(k == own_kind, 1.0, 0.0)
        kinds = kinds.astype(BF16)
        bh[0:64, lanes] = hi
        bh[64:128, lanes] = kinds
        bh[128:192, lanes] = hi
        bh[192:256, lanes] = kinds
        bl[:, lanes] = lo
        return carry

    lax.fori_loop(0, SLOTS, basis_step, 0)

    def filter_step(e, carry):
        lanes = pl.ds(pl.multiple_of(e * 256, 256), 256)
        before = mm(wcat[...], bh[:, lanes]) + mm(wcat[:, 0:64], bl[:, lanes])
        hi, lo = halves(before / (1.0 + jnp.exp(-before)))
        filt[:, lanes] = mm3(mix_hi[...], mix_lo[...], hi, lo)
        return carry

    lax.fori_loop(0, 4, filter_step, 0)
    total = sums[12]
    for k in (1, 15, 2, 14, 3, 13, 4, 12, 5, 11, 6, 10, 7, 9, 8):
        arrived(got2.at[k], r_rs2, k)
        total = total + got2[k]
    rows16[0:1, :] = total[:, 0:CH]
    rows16[1:2, :] = total[:, CH:2 * CH]
    a_hi, a_lo = halves(rows16[...])
    mixed = mm3(a_hi, a_lo, gf_hi, gf_lo)
    filt1[12, :, 0:CH] = mixed[0:1, :] * damp
    filt1[12, :, CH:2 * CH] = mixed[1:2, :] * damp
    for d in (8, 7, 9, 6, 10, 5, 11, 4, 12, 3, 13, 2, 14, 1, 15):
        at = (12 - d) % 16
        start(filt1.at[12], filt1.at[at], s_ag1, r_ag1, at, column(d), gy)

    drain()

    def spread(q):
        for k in range(8):
            at = 8 * q + k
            if at != 12:
                arrived(filt1.at[at], r_ag1, at)
            filt2[q, k:k + 1, :] = filt1[at]
        for k in PLANE_ORDER:
            start(filt2.at[q], filt3.at[q, gy], s_ag2, r_ag2, 16 * q + k, gx, plane(k))
        filt3[q, gy] = filt2[q]

    spread(1)
    spread(0)

    for i in range(3):
        arrived(halo.at[3 * i], r_halo, 2 + i)
        arrived(halo.at[3 * i + 2], r_halo, 5 + i)
    for j in range(9):
        hi, lo = halves(halo[j])
        vb[0:CH, ATOMS * j:ATOMS * j + ATOMS] = hi
        vb[CH:2 * CH, ATOMS * j:ATOMS * j + ATOMS] = lo

    def gather_step(e, acc):
        lanes = pl.ds(pl.multiple_of(e * 256, 256), 256)
        g = mm(vb[...], onehot[:, lanes])
        msg = (g[0:CH] + g[CH:2 * CH]) * filt[:, lanes]
        return acc + (msg[:, 0:ATOMS] + msg[:, ATOMS:2 * ATOMS])

    short = lax.fori_loop(0, 4, gather_step, jnp.zeros((CH, ATOMS), F32))
    out[0, 0] = jnp.transpose(short) * (1.0 / math.sqrt(SLOTS))

    def factors(q):
        for k in range(1, 16):
            sender = lax.rem(px + 4 - k // 4, 4) * 4 + lax.rem(py + 4 - k % 4, 4)
            arrived(filt3.at[q, sender], r_ag2, 16 * q + k)
        for h in range(2):
            hi, lo = halves(filt3[q, 8 * h:8 * h + 8].reshape(64, 2 * CH))
            for at, lane in ((128 * h, 0), (128 * h + 64, CH)):
                rh_hi[at:at + 64, :] = hi[:, lane:lane + CH]
                rh_lo[at:at + 64, :] = lo[:, lane:lane + CH]

    def terms(q, rows):
        return mm3(tt_hi[q, rows], tt_lo[q, rows], rh_hi[...], rh_lo[...])

    near_rows, far_rows = slice(0, ATOMS), slice(ATOMS, 2 * ATOMS)
    factors(1)
    lsum[...] = terms(1, far_rows)
    out[0, 0] += terms(1, near_rows)
    drain()
    factors(0)
    lpeer[...] = lsum[...] + terms(0, far_rows)
    start(lpeer, lgot, s_pair, r_pair, 3, peer, gy)
    base = out[0, 0] + terms(0, near_rows)
    arrived(lgot, r_pair, 3)
    out[0, 0] = base + lgot[...]
    drain()


def shards(features, offsets, species, neighbours, edge_mask, wavevectors, vw, radw, emb, mixw, gf):
    vmem = pl.BlockSpec(memory_space=pltpu.VMEM)
    hbm = pl.BlockSpec(memory_space=pltpu.HBM)
    dma = pltpu.SemaphoreType.DMA
    scratch = [
        pltpu.VMEM((ATOMS, CH), F32),
        pltpu.VMEM((3, 1, ATOMS), F32),
        pltpu.VMEM((1, 1, ATOMS), jnp.int32),
        pltpu.VMEM((SLOTS, ATOMS), jnp.int32),
        pltpu.VMEM((SLOTS, ATOMS), jnp.int32),
        pltpu.VMEM((3, MODES), jnp.int32),
        pltpu.VMEM((CH, CH), F32),
        pltpu.VMEM((2 * RADIAL, CH), F32),
        pltpu.VMEM((CH, CH), F32),
        pltpu.VMEM((CH, CH), F32),
        pltpu.VMEM((9, 8, ATOMS), F32),
        pltpu.VMEM((9, CH, ATOMS), F32),
        pltpu.VMEM((4, 128, 2 * ATOMS), F32),
        pltpu.VMEM((2, 2 * ATOMS, 256), BF16),
        pltpu.VMEM((2, 2 * ATOMS, 256), BF16),
        pltpu.VMEM((256, 128), F32),
        pltpu.VMEM((128, MODES), F32),
        pltpu.VMEM((4, 8, 8, 2 * CH), F32),
        pltpu.VMEM((4, 8, 8, 2 * CH), F32),
        pltpu.VMEM((4, 8, 8, 2 * CH), F32),
        pltpu.VMEM((2, GY, 8, 2 * CH), F32),
        pltpu.VMEM((NZ, 1, 2 * CH), F32),
        pltpu.VMEM((NZ, 1, 2 * CH), F32),
        pltpu.VMEM((16, CH), F32),
        pltpu.VMEM((NZ, 1, 2 * CH), F32),
        pltpu.VMEM((2, 8, 2 * CH), F32),
        pltpu.VMEM((2, GY, 8, 2 * CH), F32),
        pltpu.VMEM((256, CH), BF16),
        pltpu.VMEM((256, CH), BF16),
        pltpu.VMEM((ATOMS, CH), F32),
        pltpu.VMEM((ATOMS, CH), F32),
        pltpu.VMEM((ATOMS, CH), F32),
        pltpu.VMEM((SLOTS, ATOMS), F32),
        pltpu.VMEM((SLOTS, ATOMS), F32),
        pltpu.VMEM((SLOTS, ATOMS), jnp.int32),
        pltpu.VMEM((9 * ATOMS, SLOTS * ATOMS), BF16),
        pltpu.VMEM((256, SLOTS * ATOMS), BF16),
        pltpu.VMEM((64, SLOTS * ATOMS), BF16),
        pltpu.VMEM((CH, SLOTS * ATOMS), F32),
        pltpu.VMEM((CH, 256), BF16),
        pltpu.VMEM((CH, CH), BF16),
        pltpu.VMEM((CH, CH), BF16),
        pltpu.VMEM((2 * CH, 9 * ATOMS), BF16),
        pltpu.SemaphoreType.REGULAR,
        dma((11,)),
        dma((4,)), dma((4,)),
        dma((8,)), dma((8,)),
        dma((8,)), dma((8,)),
        dma((32,)), dma((32,)),
        dma((16,)), dma((16,)),
        dma((16,)), dma((16,)),
        dma((32,)), dma((32,)),
    ]
    return pl.pallas_call(
        kernel,
        out_shape=jax.ShapeDtypeStruct((1, 1, ATOMS, CH), F32),
        in_specs=[hbm] * 11,
        out_specs=vmem,
        scratch_shapes=scratch,
        compiler_params=pltpu.CompilerParams(
            collective_id=0, has_side_effects=True, vmem_limit_bytes=56 * 1024 * 1024
        ),
    )(
        features, jnp.transpose(offsets, (0, 2, 1, 3)), species, jnp.swapaxes(neighbours, 2, 3),
        jnp.swapaxes(edge_mask, 2, 3), wavevectors, vw, radw, emb, mixw, gf,
    )


def solution(mesh):
    block = P("gx", "gy", None, None)
    placed = (block, block, P("gx", "gy", None), block, block, P(), P(), P(), P(), P(), P("gx", None, None))
    return jax.shard_map(shards, mesh=mesh, in_specs=placed, out_specs=block, check_vma=False)
```

```python
import math

import jax
import jax.numpy as jnp
from jax import lax
from jax.experimental import pallas as pl
from jax.experimental.pallas import tpu as pltpu
from jax.sharding import PartitionSpec as P

MESH = pl.DeviceIdType.MESH
F32 = jnp.float32
BF16 = jnp.bfloat16

GX = 32
GY = 16
NZ = 16
ATOMS = 128
CH = 256
MODES = 512
SLOTS = 8
RADIAL = 64
SCALE = 1.0 / math.sqrt(33554432)
TURN = 2.0 * math.pi

PLANE_ORDER = (10, 9, 11, 6, 14, 8, 2, 5, 7, 13, 15, 4, 12, 1, 3)

COS_TERMS = [(-1.0) ** n * TURN ** (2 * n) / math.factorial(2 * n) for n in range(7)]

DISTANCES = [8 + 2 * q + k if k < 2 else 4 - 2 * q + k for q in range(4) for k in range(4)]
PLACE = [DISTANCES.index(d) for d in range(16)]


def halves(x):
    hi = x.astype(BF16)
    return hi, (x - hi.astype(F32)).astype(BF16)


def mm(a, b):
    return jnp.dot(a, b, preferred_element_type=F32)


def mm3(a_hi, a_lo, b_hi, b_lo):
    return mm(a_hi, b_hi) + (mm(a_hi, b_lo) + mm(a_lo, b_hi))


def cos_turns(turns):
    h = jnp.floor(turns * 2.0 + 0.5) * 0.5
    r = turns - h
    sign = 1.0 - 4.0 * (h - jnp.floor(h))
    y = r * r
    c = jnp.full_like(y, COS_TERMS[6])
    for n in range(5, -1, -1):
        c = c * y + COS_TERMS[n]
    return c * sign


def remote(src, dst, send, recv, gx, gy):
    return pltpu.make_async_remote_copy(
        src_ref=src, dst_ref=dst, send_sem=send, recv_sem=recv, device_id=(gx, gy), device_id_type=MESH
    )


def kernel(
    feat_h, offs_h, spec_h, neigh_h, mask_h, wv_h, vw_h, radw_h, emb_h, mixw_h, gf_h,
    out,
    feat, offs, spec, neigh, mask, wv, vw, embed, mixw, gf,
    near_pos, halo, tf, tt_hi, tt_lo, ncol, wpad,
    part, theirs, got0, got1, sums, got2, rows16, own_row, filt1, filt2, filt3, rh_hi, rh_lo, lsum, lpeer, lgot,
    dist, spj, rowid, onehot, bh, bl, filt, wcat, mix_hi, mix_lo, vb,
    ready, s_in, s_pair, r_pair, s_pos, r_pos, s_halo, r_halo, s_rs1, r_rs1, s_rs2, r_rs2, s_ag1, r_ag1, s_ag2, r_ag2,
):
    gx = lax.axis_index("gx")
    gy = lax.axis_index("gy")
    c = lax.rem(gx, 2)
    z = gx // 2
    px = gy // 4
    py = lax.rem(gy, 4)
    peer = gx + 1 - 2 * c
    other = lax.rem(gx + 31 + 2 * c, GX)
    up = lax.rem(gy + 1, GY)
    down = lax.rem(gy + GY - 1, GY)

    def plane(k):
        return lax.rem(px + k // 4, 4) * 4 + lax.rem(py + k % 4, 4)

    def column(k):
        return 2 * lax.rem(z + k, NZ) + c

    to_peer, to_other = 3 * (2 * c), 3 * (2 - 2 * c)
    around = [
        (peer, gy, to_peer + 1), (peer, up, to_peer), (peer, down, to_peer + 2),
        (other, gy, to_other + 1), (other, up, to_other), (other, down, to_other + 2),
        (gx, up, 3), (gx, down, 5),
    ]
    from_peer, from_other = to_other, to_peer
    slots_here = [
        from_peer + 1, from_peer, from_peer + 2, from_other + 1, from_other, from_other + 2, 3, 5,
    ]

    barrier = pltpu.get_barrier_semaphore()
    greeted = [(column(k), gy) for k in (4, 12, 3, 13, 2, 14, 1, 15)]
    greeted += [(gx, plane(k)) for k in PLANE_ORDER]
    greeted += [(other, up), (other, down), (peer, up), (peer, down), (other, gy), (peer, gy)]
    for device in greeted:
        pl.semaphore_signal(barrier, inc=1, device_id=device, device_id_type=MESH)

    loads = [
        pltpu.make_async_copy(src, dst, s_in.at[i])
        for i, (src, dst) in enumerate((
            (wv_h, wv), (offs_h.at[0], offs), (feat_h.at[0, 0], feat), (spec_h, spec), (vw_h, vw),
            (neigh_h.at[0, 0], neigh), (mask_h.at[0, 0], mask), (radw_h, embed.at[pl.ds(0, RADIAL)]),
            (emb_h, embed.at[pl.ds(RADIAL, RADIAL)]), (mixw_h, mixw), (gf_h.at[0], gf),
        ))
    ]
    for load in loads:
        load.start()
    for load in loads[0:4]:
        load.wait()
    near_pos[4] = jnp.zeros((8, ATOMS), F32)
    for i in range(3):
        near_pos[4, i:i + 1, :] = offs[i]
    near_pos[4, 3:4, :] = spec[0].astype(F32)

    wpad[...] = jnp.zeros(wpad.shape, F32)
    vectors = wv[...].astype(F32)
    wpad[0:3, :] = vectors
    even = wpad[0:8, :]
    odd = pltpu.roll(even, MODES - 16, 1)
    wpad[0:8, :] = jnp.where(c == 0, even, odd)
    wpad[8:16, :] = jnp.where(c == 0, odd, even)
    r = lax.broadcasted_iota(jnp.int32, (MODES, 1), 0)
    m = lax.broadcasted_iota(jnp.int32, (MODES, MODES), 1)
    q, k = r >> 7, r & 3
    away = jnp.where(k < 2, 8 + 2 * q, 4 - 2 * q) + k
    target = 32 * ((z + away) & 15) + ((r >> 3) & 15)
    pick = jnp.where(m == target, 1.0, 0.0).astype(BF16)
    ncol[...] = lax.dot_general(
        pick, wpad[...].astype(BF16), (((1,), (1,)), ((), ())), preferred_element_type=F32
    )

    def table(i, parity, block, positions):
        quarter = ((lax.broadcasted_iota(jnp.int32, (64, ATOMS), 0) >> 2) & 1).astype(F32) * 0.25
        rows = []
        for h in range(2):
            n = ncol[pl.ds(pl.multiple_of(i * 128 + h * 64, 64), 64), :]
            n0, n1, n2 = [n[:, 8 * parity + a:8 * parity + a + 1] for a in range(3)]
            w0 = (n0.astype(jnp.int32) * block & 31).astype(F32)
            w1 = (n1.astype(jnp.int32) * gy & 15).astype(F32)
            turns = (w0 + n0 * positions[0]) * (1.0 / 32)
            turns = turns + (w1 + n1 * positions[1]) * (1.0 / 16)
            turns = turns + n2 * positions[2]
            rows.append(cos_turns(turns - quarter))
        return jnp.concatenate(rows, axis=0)

    f_hi, f_lo = halves(feat[...])

    def own_table(i, parity, into):
        both = table(i, parity, gx, [offs[0], offs[1], offs[2]])
        t_hi, t_lo = halves(both)
        into[i] = mm3(t_hi, t_lo, f_hi, f_lo).reshape(16, 8, CH)
        return both

    def own_step(i, carry):
        own_table(i, 1, theirs)
        tf[i, :, 0:ATOMS] = own_table(i, 0, part)
        return carry

    lax.fori_loop(0, 4, own_step, 0)

    sends = []

    def start(src, dst, s_sems, r_sems, i, x, y):
        copy = remote(src, dst, s_sems.at[i], r_sems.at[i], x, y)
        copy.start()
        sends.append(copy)

    def start_all(copies, s_sems, r_sems, i, whole):
        for src, dst, x, y in copies:
            remote(src, dst, s_sems.at[i], r_sems.at[i], x, y).start()
        sends.append(remote(whole, whole, s_sems.at[i], r_sems.at[i], peer, gy))

    def arrived(dst, r_sems, i):
        remote(dst, dst, s_pair.at[0], r_sems.at[i], peer, gy).wait_recv()

    def drain():
        while sends:
            sends.pop(0).wait_send()

    pl.semaphore_wait(barrier, len(greeted))
    for k in (4, 12):
        pl.semaphore_signal(ready, inc=1, device_id=(column(k), gy), device_id_type=MESH)
    for q in range(4):
        start(theirs.at[q], got0.at[q], s_pair, r_pair, q, peer, gy)

    for i, (x, y, slot) in enumerate(around):
        start(near_pos.at[4], near_pos.at[slot], s_pos, r_pos, i, x, y)

    for q in range(4):
        arrived(got0.at[q], r_pair, q)
        part[q] = part[q] + got0[q]
        copies = [(part.at[q, plane(k)], got1.at[q, k], gx, plane(k)) for k in PLANE_ORDER]
        start_all(copies, s_rs1, r_rs1, q, got1.at[q, pl.ds(1, 15)])

    loads[4].wait()
    vw_hi, vw_lo = halves(vw[...])
    halo[4] = jnp.transpose(mm3(f_hi, f_lo, vw_hi, vw_lo))
    start(halo.at[4], halo.at[7 - 6 * c], s_halo, r_halo, 1, other, gy)
    start(halo.at[4], halo.at[1 + 6 * c], s_halo, r_halo, 0, peer, gy)
    pl.semaphore_wait(ready, 2)

    copies = []
    for q in range(4):
        arrived(got1.at[q, pl.ds(1, 15)], r_rs1, q)
        total = part[q, gy]
        for k in range(1, 16):
            total = total + got1[q, k]
        for k in range(4):
            sums[4 * q + k, 0:1, :] = total[k:k + 1, :]
            sums[4 * q + k, 1:2, :] = total[4 + k:5 + k, :]
        for k in (0, 1, 3, 2):
            d = DISTANCES[4 * q + k]
            if d:
                remote(
                    sums.at[4 * q + k], got2.at[d], s_rs2.at[0], r_rs2.at[0], column(d), gy
                ).start()
    sends.append(remote(got2.at[pl.ds(1, 15)], got2.at[pl.ds(1, 15)], s_rs2.at[0], r_rs2.at[0], peer, gy))

    arrived(halo.at[7 - 6 * c], r_halo, 0)
    arrived(halo.at[1 + 6 * c], r_halo, 1)
    for i in range(3):
        start(halo.at[3 * i + 1], halo.at[3 * i], s_halo, r_halo, 2 + i, gx, up)
        start(halo.at[3 * i + 1], halo.at[3 * i + 2], s_halo, r_halo, 5 + i, gx, down)

    for load in loads[5:]:
        load.wait()
    mine = lax.broadcasted_iota(jnp.int32, (3, MODES), 1) == gx * 16 + gy
    wave = jnp.sum(jnp.where(mine, vectors, 0.0), axis=1, keepdims=True)
    wave0 = wave[0:1] * (TURN / 32)
    wave1 = wave[1:2] * (TURN / 16)
    wave2 = wave[2:3] * TURN
    damp = jnp.exp(-0.01 * (wave0 * wave0 + wave1 * wave1 + wave2 * wave2)) * SCALE
    gf_hi, gf_lo = halves(gf[...])
    rows16[...] = jnp.zeros(rows16.shape, F32)

    for i, slot in enumerate(slots_here):
        arrived(near_pos.at[slot], r_pos, i)

    def peer_step(i, carry):
        there = near_pos[from_peer + 1]
        tf[i, :, ATOMS:2 * ATOMS] = table(i, 0, peer, [there[0:1], there[1:2], there[2:3]])
        return carry

    lax.fori_loop(0, 4, peer_step, 0)
    for i in range(4):
        hi, lo = halves(jnp.transpose(tf[i]))
        tt_hi[i] = hi
        tt_lo[i] = lo
    wt = jnp.transpose(embed[...])
    hi, lo = halves(wt)
    wcat[:, 0:128] = hi
    wcat[:, 128:256] = lo
    hi, lo = halves(jnp.transpose(mixw[...]))
    mix_hi[...] = hi
    mix_lo[...] = lo

    listed = jnp.where(mask[...] > 0, neigh[...], -1)
    source = listed >> 7
    atom = listed & 127
    s = (((source >> 4) - gx + 1) & 31) - 1
    t = (((source & 15) - gy + 1) & 15) - 1
    near = (s + 1) * 3 + (t + 1)
    rowid[...] = jnp.where(listed < 0, -1, near * ATOMS + atom)

    def onehot_step(e, carry):
        lanes = pl.ds(pl.multiple_of(e * ATOMS, ATOMS), ATOMS)
        place = rowid[pl.ds(e, 1), :]
        at = lax.broadcasted_iota(jnp.int32, (ATOMS, ATOMS), 0)
        for j in range(9):
            hit = jnp.where(at == place - ATOMS * j, 1.0, 0.0)
            onehot[ATOMS * j:ATOMS * j + ATOMS, lanes] = hit.astype(BF16)
        return carry

    lax.fori_loop(0, SLOTS, onehot_step, 0)

    found = [jnp.zeros((SLOTS, ATOMS), F32) for _ in range(4)]
    for j in range(9):
        for i in range(4):
            row = jnp.broadcast_to(near_pos[j, i:i + 1, :], (SLOTS, ATOMS))
            taken = jnp.take_along_axis(row, atom, axis=1)
            found[i] = jnp.where(near == j, taken, found[i])
    own = near_pos[4]
    gap0 = (s.astype(F32) + found[0]) - own[0:1, :]
    gap1 = (t.astype(F32) + found[1]) - own[1:2, :]
    gap2 = found[2] - own[2:3, :]
    dist[...] = jnp.sqrt(gap0 * gap0 + gap1 * gap1 + gap2 * gap2 + 0.01)
    spj[...] = found[3]
    own_kind = own[3:4, :]

    def basis_step(e, carry):
        lanes = pl.ds(pl.multiple_of(e * ATOMS, ATOMS), ATOMS)
        k = lax.broadcasted_iota(jnp.int32, (RADIAL, ATOMS), 0).astype(F32)
        scaled = (dist[pl.ds(e, 1), :] - k * (3.0 / 63)) / (6.0 / 63)
        hi, lo = halves(jnp.exp(-scaled * scaled))
        kinds = jnp.where(k == spj[pl.ds(e, 1), :], 1.0, 0.0) + jnp.where(k == own_kind, 1.0, 0.0)
        kinds = kinds.astype(BF16)
        bh[0:64, lanes] = hi
        bh[64:128, lanes] = kinds
        bh[128:192, lanes] = hi
        bh[192:256, lanes] = kinds
        bl[:, lanes] = lo
        return carry

    lax.fori_loop(0, SLOTS, basis_step, 0)

    def filter_step(e, carry):
        lanes = pl.ds(pl.multiple_of(e * 256, 256), 256)
        before = mm(wcat[...], bh[:, lanes]) + mm(wcat[:, 0:64], bl[:, lanes])
        hi, lo = halves(before / (1.0 + jnp.exp(-before)))
        filt[:, lanes] = mm3(mix_hi[...], mix_lo[...], hi, lo)
        return carry

    lax.fori_loop(0, 4, filter_step, 0)
    arrived(got2.at[pl.ds(1, 15)], r_rs2, 0)
    total = sums[PLACE[0]]
    for k in range(1, 16):
        total = total + got2[k]
    rows16[0:2, :] = total
    a_hi, a_lo = halves(rows16[...])
    mixed = mm3(a_hi, a_lo, gf_hi, gf_lo)
    own_row[0] = mixed[0:2, :] * damp
    for d in (8, 7, 9, 6, 10, 5, 11, 4, 12, 3, 13, 2, 14, 1, 15):
        at = PLACE[16 - d]
        remote(own_row.at[0], filt1.at[at], s_ag1.at[0], r_ag1.at[at // 4], column(d), gy).start()
    sends.append(remote(got2.at[pl.ds(1, 15)], got2.at[pl.ds(1, 15)], s_ag1.at[0], r_ag1.at[0], peer, gy))

    drain()

    for q in (3, 2, 1, 0):
        arrived(filt1.at[pl.ds(4 * q, 4 if q < 3 else 3)], r_ag1, q)
        for k in range(4):
            at = 4 * q + k
            row = own_row.at[0] if at == PLACE[0] else filt1.at[at]
            filt2[q, k:k + 1, :] = row[0:1, :]
            filt2[q, 4 + k:5 + k, :] = row[1:2, :]
        copies = [(filt2.at[q], filt3.at[q, gy], gx, plane(k)) for k in PLANE_ORDER]
        start_all(copies, s_ag2, r_ag2, q, got1.at[q, pl.ds(1, 15)])
        filt3[q, gy] = filt2[q]

    for i in range(3):
        arrived(halo.at[3 * i], r_halo, 2 + i)
        arrived(halo.at[3 * i + 2], r_halo, 5 + i)
    for j in range(9):
        hi, lo = halves(halo[j])
        vb[0:CH, ATOMS * j:ATOMS * j + ATOMS] = hi
        vb[CH:2 * CH, ATOMS * j:ATOMS * j + ATOMS] = lo

    def gather_step(e, acc):
        lanes = pl.ds(pl.multiple_of(e * 256, 256), 256)
        g = mm(vb[...], onehot[:, lanes])
        msg = (g[0:CH] + g[CH:2 * CH]) * filt[:, lanes]
        return acc + (msg[:, 0:ATOMS] + msg[:, ATOMS:2 * ATOMS])

    short = lax.fori_loop(0, 4, gather_step, jnp.zeros((CH, ATOMS), F32))
    out[0, 0] = jnp.transpose(short) * (1.0 / math.sqrt(SLOTS))

    def factors(q):
        arrived(filt3.at[q, pl.ds(0, 15)], r_ag2, q)
        hi, lo = halves(filt3[q].reshape(128, CH))
        rh_hi[...] = hi
        rh_lo[...] = lo

    def terms(q, rows):
        return mm3(tt_hi[q, rows], tt_lo[q, rows], rh_hi[...], rh_lo[...])

    near_rows, far_rows = slice(0, ATOMS), slice(ATOMS, 2 * ATOMS)
    for q in (3, 2, 1):
        factors(q)
        lsum[...] = terms(q, far_rows) + (lsum[...] if q < 3 else 0.0)
        out[0, 0] += terms(q, near_rows)
    drain()
    factors(0)
    lpeer[...] = lsum[...] + terms(0, far_rows)
    start(lpeer, lgot, s_pair, r_pair, 4, peer, gy)
    base = out[0, 0] + terms(0, near_rows)
    arrived(lgot, r_pair, 4)
    out[0, 0] = base + lgot[...]
    drain()


def shards(features, offsets, species, neighbours, edge_mask, wavevectors, vw, radw, emb, mixw, gf):
    vmem = pl.BlockSpec(memory_space=pltpu.VMEM)
    hbm = pl.BlockSpec(memory_space=pltpu.HBM)
    dma = pltpu.SemaphoreType.DMA
    scratch = [
        pltpu.VMEM((ATOMS, CH), F32),
        pltpu.VMEM((3, 1, ATOMS), F32),
        pltpu.VMEM((1, 1, ATOMS), jnp.int32),
        pltpu.VMEM((SLOTS, ATOMS), jnp.int32),
        pltpu.VMEM((SLOTS, ATOMS), jnp.int32),
        pltpu.VMEM((3, MODES), jnp.int32),
        pltpu.VMEM((CH, CH), F32),
        pltpu.VMEM((2 * RADIAL, CH), F32),
        pltpu.VMEM((CH, CH), F32),
        pltpu.VMEM((CH, CH), F32),
        pltpu.VMEM((9, 8, ATOMS), F32),
        pltpu.VMEM((9, CH, ATOMS), F32),
        pltpu.VMEM((4, 128, 2 * ATOMS), F32),
        pltpu.VMEM((4, 2 * ATOMS, 128), BF16),
        pltpu.VMEM((4, 2 * ATOMS, 128), BF16),
        pltpu.VMEM((MODES, 128), F32),
        pltpu.VMEM((128, MODES), F32),
        pltpu.VMEM((4, GY, 8, CH), F32),
        pltpu.VMEM((4, GY, 8, CH), F32),
        pltpu.VMEM((4, GY, 8, CH), F32),
        pltpu.VMEM((4, GY, 8, CH), F32),
        pltpu.VMEM((NZ, 2, CH), F32),
        pltpu.VMEM((NZ, 2, CH), F32),
        pltpu.VMEM((16, CH), F32),
        pltpu.VMEM((1, 2, CH), F32),
        pltpu.VMEM((NZ, 2, CH), F32),
        pltpu.VMEM((4, 8, CH), F32),
        pltpu.VMEM((4, GY, 8, CH), F32),
        pltpu.VMEM((128, CH), BF16),
        pltpu.VMEM((128, CH), BF16),
        pltpu.VMEM((ATOMS, CH), F32),
        pltpu.VMEM((ATOMS, CH), F32),
        pltpu.VMEM((ATOMS, CH), F32),
        pltpu.VMEM((SLOTS, ATOMS), F32),
        pltpu.VMEM((SLOTS, ATOMS), F32),
        pltpu.VMEM((SLOTS, ATOMS), jnp.int32),
        pltpu.VMEM((9 * ATOMS, SLOTS * ATOMS), BF16),
        pltpu.VMEM((256, SLOTS * ATOMS), BF16),
        pltpu.VMEM((64, SLOTS * ATOMS), BF16),
        pltpu.VMEM((CH, SLOTS * ATOMS), F32),
        pltpu.VMEM((CH, 256), BF16),
        pltpu.VMEM((CH, CH), BF16),
        pltpu.VMEM((CH, CH), BF16),
        pltpu.VMEM((2 * CH, 9 * ATOMS), BF16),
        pltpu.SemaphoreType.REGULAR,
        dma((11,)),
        dma((5,)), dma((5,)),
        dma((8,)), dma((8,)),
        dma((8,)), dma((8,)),
        dma((4,)), dma((4,)),
        dma((1,)), dma((1,)),
        dma((1,)), dma((4,)),
        dma((4,)), dma((4,)),
    ]
    return pl.pallas_call(
        kernel,
        out_shape=jax.ShapeDtypeStruct((1, 1, ATOMS, CH), F32),
        in_specs=[hbm] * 11,
        out_specs=vmem,
        scratch_shapes=scratch,
        compiler_params=pltpu.CompilerParams(
            collective_id=0, has_side_effects=True, vmem_limit_bytes=56 * 1024 * 1024
        ),
    )(
        features, jnp.transpose(offsets, (0, 2, 1, 3)), species, jnp.swapaxes(neighbours, 2, 3),
        jnp.swapaxes(edge_mask, 2, 3), wavevectors, vw, radw, emb, mixw, gf,
    )


def solution(mesh):
    block = P("gx", "gy", None, None)
    placed = (block, block, P("gx", "gy", None), block, block, P(), P(), P(), P(), P(), P("gx", None, None))
    return jax.shard_map(shards, mesh=mesh, in_specs=placed, out_specs=block, check_vma=False)
```

```python
import math

import jax
import jax.numpy as jnp
from jax import lax
from jax.experimental import pallas as pl
from jax.experimental.pallas import tpu as pltpu
from jax.sharding import PartitionSpec as P

MESH = pl.DeviceIdType.MESH
F32 = jnp.float32
BF16 = jnp.bfloat16

GX = 32
GY = 16
NZ = 16
ATOMS = 128
CH = 256
MODES = 512
SLOTS = 8
RADIAL = 64
SCALE = 1.0 / math.sqrt(33554432)
TURN = 2.0 * math.pi

PLANE_ORDER = (10, 9, 11, 6, 14, 8, 2, 5, 7, 13, 15, 4, 12, 1, 3)

COS_TERMS = [(-1.0) ** n * TURN ** (2 * n) / math.factorial(2 * n) for n in range(7)]

DISTANCES = [8 + 2 * q + k if k < 2 else 4 - 2 * q + k for q in range(4) for k in range(4)]
PLACE = [DISTANCES.index(d) for d in range(16)]


def halves(x):
    hi = x.astype(BF16)
    return hi, (x - hi.astype(F32)).astype(BF16)


def mm(a, b):
    return jnp.dot(a, b, preferred_element_type=F32)


def mm3(a_hi, a_lo, b_hi, b_lo):
    return mm(a_hi, b_hi) + (mm(a_hi, b_lo) + mm(a_lo, b_hi))


def cos_turns(turns):
    h = jnp.floor(turns * 2.0 + 0.5) * 0.5
    r = turns - h
    sign = 1.0 - 4.0 * (h - jnp.floor(h))
    y = r * r
    c = jnp.full_like(y, COS_TERMS[6])
    for n in range(5, -1, -1):
        c = c * y + COS_TERMS[n]
    return c * sign


def stacked(hi_lo, b_hi, b_lo):
    rows = hi_lo.shape[0] // 2
    upper = mm(hi_lo, b_hi)
    return upper[0:rows] + (upper[rows:] + mm(hi_lo[0:rows], b_lo))


def remote(src, dst, send, recv, gx, gy):
    return pltpu.make_async_remote_copy(
        src_ref=src, dst_ref=dst, send_sem=send, recv_sem=recv, device_id=(gx, gy), device_id_type=MESH
    )


def kernel(
    feat_h, offs_h, spec_h, neigh_h, mask_h, wv_h, vw_h, radw_h, emb_h, mixw_h, gf_h,
    out,
    feat, offs, spec, neigh, mask, wv, vw, embed, mixw, gf,
    near_pos, halo, tf, tt, ncol, wpad,
    part, theirs, got0, got1, sums, got2, rows16, own_row, filt1, filt2, filt3, rh_hi, rh_lo, lsum, lpeer, lgot,
    dist, spj, rowid, onehot, bh, bl, filt, wcat, mix_hi, mix_lo, vb,
    ready, s_in, s_pair, r_pair, s_pos, r_pos, s_halo, r_halo, s_rs1, r_rs1, s_rs2, r_rs2, s_ag1, r_ag1, s_ag2, r_ag2,
):
    gx = lax.axis_index("gx")
    gy = lax.axis_index("gy")
    c = lax.rem(gx, 2)
    z = gx // 2
    px = gy // 4
    py = lax.rem(gy, 4)
    peer = gx + 1 - 2 * c
    other = lax.rem(gx + 31 + 2 * c, GX)
    up = lax.rem(gy + 1, GY)
    down = lax.rem(gy + GY - 1, GY)

    def plane(k):
        return lax.rem(px + k // 4, 4) * 4 + lax.rem(py + k % 4, 4)

    def column(k):
        return 2 * lax.rem(z + k, NZ) + c

    to_peer, to_other = 3 * (2 * c), 3 * (2 - 2 * c)
    around = [
        (peer, gy, to_peer + 1), (peer, up, to_peer), (peer, down, to_peer + 2),
        (other, gy, to_other + 1), (other, up, to_other), (other, down, to_other + 2),
        (gx, up, 3), (gx, down, 5),
    ]
    from_peer, from_other = to_other, to_peer
    slots_here = [
        from_peer + 1, from_peer, from_peer + 2, from_other + 1, from_other, from_other + 2, 3, 5,
    ]

    barrier = pltpu.get_barrier_semaphore()
    greeted = [(gx, plane(10)), (column(4), gy), (column(12), gy)]
    greeted += [(gx, plane(k)) for k in PLANE_ORDER[1:5]] + [(other, up), (other, down)]
    greeted += [(column(3), gy), (column(13), gy), (peer, up), (peer, down)]
    greeted += [(gx, plane(k)) for k in PLANE_ORDER[5:11]] + [(column(2), gy), (column(14), gy)]
    greeted += [(gx, plane(k)) for k in PLANE_ORDER[11:]] + [(column(1), gy), (column(15), gy)]
    greeted += [(other, gy), (peer, gy)]
    for device in greeted:
        pl.semaphore_signal(barrier, inc=1, device_id=device, device_id_type=MESH)

    loads = [
        pltpu.make_async_copy(src, dst, s_in.at[i])
        for i, (src, dst) in enumerate((
            (wv_h, wv), (offs_h.at[0], offs), (feat_h.at[0, 0], feat), (spec_h, spec), (vw_h, vw),
            (neigh_h.at[0, 0], neigh), (mask_h.at[0, 0], mask), (radw_h, embed.at[pl.ds(0, RADIAL)]),
            (emb_h, embed.at[pl.ds(RADIAL, RADIAL)]), (mixw_h, mixw), (gf_h.at[0], gf),
        ))
    ]
    for load in loads:
        load.start()
    for load in loads[0:4]:
        load.wait()
    near_pos[4] = jnp.zeros((8, ATOMS), F32)
    for i in range(3):
        near_pos[4, i:i + 1, :] = offs[i]
    near_pos[4, 3:4, :] = spec[0].astype(F32)

    wpad[...] = jnp.zeros(wpad.shape, F32)
    vectors = wv[...].astype(F32)
    wpad[0:3, :] = vectors
    even = wpad[0:8, :]
    odd = pltpu.roll(even, MODES - 16, 1)
    wpad[0:8, :] = jnp.where(c == 0, even, odd)
    wpad[8:16, :] = jnp.where(c == 0, odd, even)
    r = lax.broadcasted_iota(jnp.int32, (MODES, 1), 0)
    m = lax.broadcasted_iota(jnp.int32, (MODES, MODES), 1)
    q, k = r >> 7, r & 3
    away = jnp.where(k < 2, 8 + 2 * q, 4 - 2 * q) + k
    target = 32 * ((z + away) & 15) + ((r >> 3) & 15)
    pick = jnp.where(m == target, 1.0, 0.0).astype(BF16)
    ncol[...] = lax.dot_general(
        pick, wpad[...].astype(BF16), (((1,), (1,)), ((), ())), preferred_element_type=F32
    )

    def table(i, parity, block, positions):
        quarter = ((lax.broadcasted_iota(jnp.int32, (64, ATOMS), 0) >> 2) & 1).astype(F32) * 0.25
        rows = []
        for h in range(2):
            n = ncol[pl.ds(pl.multiple_of(i * 128 + h * 64, 64), 64), :]
            n0, n1, n2 = [n[:, 8 * parity + a:8 * parity + a + 1] for a in range(3)]
            w0 = (n0.astype(jnp.int32) * block & 31).astype(F32)
            w1 = (n1.astype(jnp.int32) * gy & 15).astype(F32)
            turns = (w0 + n0 * positions[0]) * (1.0 / 32)
            turns = turns + (w1 + n1 * positions[1]) * (1.0 / 16)
            turns = turns + n2 * positions[2]
            rows.append(cos_turns(turns - quarter))
        return jnp.concatenate(rows, axis=0)

    f_hi, f_lo = halves(feat[...])

    def own_table(i, parity, into):
        both = table(i, parity, gx, [offs[0], offs[1], offs[2]])
        t_hi, t_lo = halves(both)
        into[i] = mm3(t_hi, t_lo, f_hi, f_lo).reshape(16, 8, CH)
        return both

    def own_step(i, carry):
        own_table(i, 1, theirs)
        tf[i, :, 0:ATOMS] = own_table(i, 0, part)
        return carry

    lax.fori_loop(0, 4, own_step, 0)

    sends = []

    def start(src, dst, s_sems, r_sems, i, x, y):
        copy = remote(src, dst, s_sems.at[i], r_sems.at[i], x, y)
        copy.start()
        sends.append(copy)

    def start_all(copies, s_sems, r_sems, i, whole):
        for src, dst, x, y in copies:
            remote(src, dst, s_sems.at[i], r_sems.at[i], x, y).start()
        sends.append(remote(whole, whole, s_sems.at[i], r_sems.at[i], peer, gy))

    def arrived(dst, r_sems, i):
        remote(dst, dst, s_pair.at[0], r_sems.at[i], peer, gy).wait_recv()

    def drain():
        while sends:
            sends.pop(0).wait_send()

    pl.semaphore_wait(barrier, len(greeted))
    for k in (4, 12):
        pl.semaphore_signal(ready, inc=1, device_id=(column(k), gy), device_id_type=MESH)
    for q in range(4):
        start(theirs.at[q], got0.at[q], s_pair, r_pair, q, peer, gy)

    for i, (x, y, slot) in enumerate(around):
        start(near_pos.at[4], near_pos.at[slot], s_pos, r_pos, i, x, y)

    for q in range(4):
        arrived(got0.at[q], r_pair, q)
        part[q] = part[q] + got0[q]
        copies = [(part.at[q, plane(k)], got1.at[q, k], gx, plane(k)) for k in PLANE_ORDER]
        start_all(copies, s_rs1, r_rs1, q, got1.at[q, pl.ds(1, 15)])

    loads[4].wait()
    vw_hi, vw_lo = halves(vw[...])
    halo[4] = jnp.transpose(mm3(f_hi, f_lo, vw_hi, vw_lo))
    start(halo.at[4], halo.at[7 - 6 * c], s_halo, r_halo, 1, other, gy)
    start(halo.at[4], halo.at[1 + 6 * c], s_halo, r_halo, 0, peer, gy)
    pl.semaphore_wait(ready, 2)

    copies = []
    for q in range(4):
        arrived(got1.at[q, pl.ds(1, 15)], r_rs1, q)
        total = part[q, gy]
        for k in range(1, 16):
            total = total + got1[q, k]
        for k in range(4):
            sums[4 * q + k, 0:1, :] = total[k:k + 1, :]
            sums[4 * q + k, 1:2, :] = total[4 + k:5 + k, :]
        for k in (0, 1, 3, 2):
            d = DISTANCES[4 * q + k]
            if d:
                remote(
                    sums.at[4 * q + k], got2.at[d], s_rs2.at[0], r_rs2.at[0], column(d), gy
                ).start()
    sends.append(remote(got2.at[pl.ds(1, 15)], got2.at[pl.ds(1, 15)], s_rs2.at[0], r_rs2.at[0], peer, gy))

    arrived(halo.at[7 - 6 * c], r_halo, 0)
    arrived(halo.at[1 + 6 * c], r_halo, 1)
    for i in range(3):
        start(halo.at[3 * i + 1], halo.at[3 * i], s_halo, r_halo, 2 + i, gx, up)
        start(halo.at[3 * i + 1], halo.at[3 * i + 2], s_halo, r_halo, 5 + i, gx, down)

    for load in loads[5:]:
        load.wait()
    mine = lax.broadcasted_iota(jnp.int32, (3, MODES), 1) == gx * 16 + gy
    wave = jnp.sum(jnp.where(mine, vectors, 0.0), axis=1, keepdims=True)
    wave0 = wave[0:1] * (TURN / 32)
    wave1 = wave[1:2] * (TURN / 16)
    wave2 = wave[2:3] * TURN
    damp = jnp.exp(-0.01 * (wave0 * wave0 + wave1 * wave1 + wave2 * wave2)) * SCALE
    gf_hi, gf_lo = halves(gf[...])
    rows16[...] = jnp.zeros(rows16.shape, F32)

    for i, slot in enumerate(slots_here):
        arrived(near_pos.at[slot], r_pos, i)

    def peer_step(i, carry):
        there = near_pos[from_peer + 1]
        tf[i, :, ATOMS:2 * ATOMS] = table(i, 0, peer, [there[0:1], there[1:2], there[2:3]])
        return carry

    lax.fori_loop(0, 4, peer_step, 0)
    for i in range(4):
        hi, lo = halves(jnp.transpose(tf[i]))
        for at, rows in ((0, slice(ATOMS, 2 * ATOMS)), (2 * ATOMS, slice(0, ATOMS))):
            tt[i, at:at + ATOMS, :] = hi[rows]
            tt[i, at + ATOMS:at + 2 * ATOMS, :] = lo[rows]
    wt = jnp.transpose(embed[...])
    hi, lo = halves(wt)
    wcat[:, 0:128] = hi
    wcat[:, 128:256] = lo
    hi, lo = halves(jnp.transpose(mixw[...]))
    mix_hi[...] = hi
    mix_lo[...] = lo

    listed = jnp.where(mask[...] > 0, neigh[...], -1)
    source = listed >> 7
    atom = listed & 127
    s = (((source >> 4) - gx + 1) & 31) - 1
    t = (((source & 15) - gy + 1) & 15) - 1
    near = (s + 1) * 3 + (t + 1)
    rowid[...] = jnp.where(listed < 0, -1, near * ATOMS + atom)

    def onehot_step(e, carry):
        lanes = pl.ds(pl.multiple_of(e * ATOMS, ATOMS), ATOMS)
        place = rowid[pl.ds(e, 1), :]
        at = lax.broadcasted_iota(jnp.int32, (ATOMS, ATOMS), 0)
        for j in range(9):
            hit = jnp.where(at == place - ATOMS * j, 1.0, 0.0)
            onehot[ATOMS * j:ATOMS * j + ATOMS, lanes] = hit.astype(BF16)
        return carry

    lax.fori_loop(0, SLOTS, onehot_step, 0)

    found = [jnp.zeros((SLOTS, ATOMS), F32) for _ in range(4)]
    for j in range(9):
        for i in range(4):
            row = jnp.broadcast_to(near_pos[j, i:i + 1, :], (SLOTS, ATOMS))
            taken = jnp.take_along_axis(row, atom, axis=1)
            found[i] = jnp.where(near == j, taken, found[i])
    own = near_pos[4]
    gap0 = (s.astype(F32) + found[0]) - own[0:1, :]
    gap1 = (t.astype(F32) + found[1]) - own[1:2, :]
    gap2 = found[2] - own[2:3, :]
    dist[...] = jnp.sqrt(gap0 * gap0 + gap1 * gap1 + gap2 * gap2 + 0.01)
    spj[...] = found[3]
    own_kind = own[3:4, :]

    def basis_step(e, carry):
        lanes = pl.ds(pl.multiple_of(e * ATOMS, ATOMS), ATOMS)
        k = lax.broadcasted_iota(jnp.int32, (RADIAL, ATOMS), 0).astype(F32)
        scaled = (dist[pl.ds(e, 1), :] - k * (3.0 / 63)) / (6.0 / 63)
        hi, lo = halves(jnp.exp(-scaled * scaled))
        kinds = jnp.where(k == spj[pl.ds(e, 1), :], 1.0, 0.0) + jnp.where(k == own_kind, 1.0, 0.0)
        kinds = kinds.astype(BF16)
        bh[0:64, lanes] = hi
        bh[64:128, lanes] = kinds
        bh[128:192, lanes] = hi
        bh[192:256, lanes] = kinds
        bl[:, lanes] = lo
        return carry

    lax.fori_loop(0, SLOTS, basis_step, 0)

    def filter_step(e, carry):
        lanes = pl.ds(pl.multiple_of(e * 256, 256), 256)
        before = mm(wcat[...], bh[:, lanes]) + mm(wcat[:, 0:64], bl[:, lanes])
        hi, lo = halves(before / (1.0 + jnp.exp(-before)))
        filt[:, lanes] = mm3(mix_hi[...], mix_lo[...], hi, lo)
        return carry

    lax.fori_loop(0, 4, filter_step, 0)
    arrived(got2.at[pl.ds(1, 15)], r_rs2, 0)
    total = sums[PLACE[0]]
    for k in range(1, 16):
        total = total + got2[k]
    rows16[0:2, :] = total
    mixed = stacked(jnp.concatenate(halves(rows16[...]), axis=0), gf_hi, gf_lo)
    own_row[0] = mixed[0:2, :] * damp
    for d in (8, 7, 9, 6, 10, 5, 11, 4, 12, 3, 13, 2, 14, 1, 15):
        at = PLACE[16 - d]
        remote(own_row.at[0], filt1.at[at], s_ag1.at[0], r_ag1.at[at // 4], column(d), gy).start()
    sends.append(remote(got2.at[pl.ds(1, 15)], got2.at[pl.ds(1, 15)], s_ag1.at[0], r_ag1.at[0], peer, gy))

    drain()

    for q in (3, 2, 1, 0):
        arrived(filt1.at[pl.ds(4 * q, 4 if q < 3 else 3)], r_ag1, q)
        for k in range(4):
            at = 4 * q + k
            row = own_row.at[0] if at == PLACE[0] else filt1.at[at]
            filt2[q, k:k + 1, :] = row[0:1, :]
            filt2[q, 4 + k:5 + k, :] = row[1:2, :]
        copies = [(filt2.at[q], filt3.at[q, gy], gx, plane(k)) for k in PLANE_ORDER]
        start_all(copies, s_ag2, r_ag2, q, got1.at[q, pl.ds(1, 15)])
        filt3[q, gy] = filt2[q]

    for i in range(3):
        arrived(halo.at[3 * i], r_halo, 2 + i)
        arrived(halo.at[3 * i + 2], r_halo, 5 + i)
    for j in range(9):
        hi, lo = halves(halo[j])
        vb[0:CH, ATOMS * j:ATOMS * j + ATOMS] = hi
        vb[CH:2 * CH, ATOMS * j:ATOMS * j + ATOMS] = lo

    def gather_step(e, acc):
        lanes = pl.ds(pl.multiple_of(e * 256, 256), 256)
        g = mm(vb[...], onehot[:, lanes])
        msg = (g[0:CH] + g[CH:2 * CH]) * filt[:, lanes]
        return acc + (msg[:, 0:ATOMS] + msg[:, ATOMS:2 * ATOMS])

    short = lax.fori_loop(0, 4, gather_step, jnp.zeros((CH, ATOMS), F32))
    out[0, 0] = jnp.transpose(short) * (1.0 / math.sqrt(SLOTS))

    def factors(q):
        arrived(filt3.at[q, pl.ds(0, 15)], r_ag2, q)
        hi, lo = halves(filt3[q].reshape(128, CH))
        rh_hi[...] = hi
        rh_lo[...] = lo

    def terms(q, rows):
        return stacked(tt[q, rows], rh_hi[...], rh_lo[...])

    near_rows, far_rows = slice(2 * ATOMS, 4 * ATOMS), slice(0, 2 * ATOMS)
    for q in (3, 2, 1):
        factors(q)
        lsum[...] = terms(q, far_rows) + (lsum[...] if q < 3 else 0.0)
        out[0, 0] += terms(q, near_rows)
    drain()
    factors(0)
    lpeer[...] = lsum[...] + terms(0, far_rows)
    start(lpeer, lgot, s_pair, r_pair, 4, peer, gy)
    base = out[0, 0] + terms(0, near_rows)
    arrived(lgot, r_pair, 4)
    out[0, 0] = base + lgot[...]
    drain()


def shards(features, offsets, species, neighbours, edge_mask, wavevectors, vw, radw, emb, mixw, gf):
    vmem = pl.BlockSpec(memory_space=pltpu.VMEM)
    hbm = pl.BlockSpec(memory_space=pltpu.HBM)
    dma = pltpu.SemaphoreType.DMA
    scratch = [
        pltpu.VMEM((ATOMS, CH), F32),
        pltpu.VMEM((3, 1, ATOMS), F32),
        pltpu.VMEM((1, 1, ATOMS), jnp.int32),
        pltpu.VMEM((SLOTS, ATOMS), jnp.int32),
        pltpu.VMEM((SLOTS, ATOMS), jnp.int32),
        pltpu.VMEM((3, MODES), jnp.int32),
        pltpu.VMEM((CH, CH), F32),
        pltpu.VMEM((2 * RADIAL, CH), F32),
        pltpu.VMEM((CH, CH), F32),
        pltpu.VMEM((CH, CH), F32),
        pltpu.VMEM((9, 8, ATOMS), F32),
        pltpu.VMEM((9, CH, ATOMS), F32),
        pltpu.VMEM((4, 128, 2 * ATOMS), F32),
        pltpu.VMEM((4, 4 * ATOMS, 128), BF16),
        pltpu.VMEM((MODES, 128), F32),
        pltpu.VMEM((128, MODES), F32),
        pltpu.VMEM((4, GY, 8, CH), F32),
        pltpu.VMEM((4, GY, 8, CH), F32),
        pltpu.VMEM((4, GY, 8, CH), F32),
        pltpu.VMEM((4, GY, 8, CH), F32),
        pltpu.VMEM((NZ, 2, CH), F32),
        pltpu.VMEM((NZ, 2, CH), F32),
        pltpu.VMEM((16, CH), F32),
        pltpu.VMEM((1, 2, CH), F32),
        pltpu.VMEM((NZ, 2, CH), F32),
        pltpu.VMEM((4, 8, CH), F32),
        pltpu.VMEM((4, GY, 8, CH), F32),
        pltpu.VMEM((128, CH), BF16),
        pltpu.VMEM((128, CH), BF16),
        pltpu.VMEM((ATOMS, CH), F32),
        pltpu.VMEM((ATOMS, CH), F32),
        pltpu.VMEM((ATOMS, CH), F32),
        pltpu.VMEM((SLOTS, ATOMS), F32),
        pltpu.VMEM((SLOTS, ATOMS), F32),
        pltpu.VMEM((SLOTS, ATOMS), jnp.int32),
        pltpu.VMEM((9 * ATOMS, SLOTS * ATOMS), BF16),
        pltpu.VMEM((256, SLOTS * ATOMS), BF16),
        pltpu.VMEM((64, SLOTS * ATOMS), BF16),
        pltpu.VMEM((CH, SLOTS * ATOMS), F32),
        pltpu.VMEM((CH, 256), BF16),
        pltpu.VMEM((CH, CH), BF16),
        pltpu.VMEM((CH, CH), BF16),
        pltpu.VMEM((2 * CH, 9 * ATOMS), BF16),
        pltpu.SemaphoreType.REGULAR,
        dma((11,)),
        dma((5,)), dma((5,)),
        dma((8,)), dma((8,)),
        dma((8,)), dma((8,)),
        dma((4,)), dma((4,)),
        dma((1,)), dma((1,)),
        dma((1,)), dma((4,)),
        dma((4,)), dma((4,)),
    ]
    return pl.pallas_call(
        kernel,
        out_shape=jax.ShapeDtypeStruct((1, 1, ATOMS, CH), F32),
        in_specs=[hbm] * 11,
        out_specs=vmem,
        scratch_shapes=scratch,
        compiler_params=pltpu.CompilerParams(
            collective_id=0, has_side_effects=True, vmem_limit_bytes=40 * 1024 * 1024
        ),
    )(*[pltpu.with_memory_space_constraint(x, pltpu.HBM) for x in (
        features, jnp.transpose(offsets, (0, 2, 1, 3)), species, jnp.swapaxes(neighbours, 2, 3),
        jnp.swapaxes(edge_mask, 2, 3), wavevectors, vw, radw, emb, mixw, gf,
    )])


def solution(mesh):
    block = P("gx", "gy", None, None)
    placed = (block, block, P("gx", "gy", None), block, block, P(), P(), P(), P(), P(), P("gx", None, None))
    return jax.shard_map(shards, mesh=mesh, in_specs=placed, out_specs=block, check_vma=False)
```

```python
import math

import jax
import jax.numpy as jnp
from jax import lax
from jax.experimental import pallas as pl
from jax.experimental.pallas import tpu as pltpu
from jax.sharding import PartitionSpec as P

MESH = pl.DeviceIdType.MESH
F32 = jnp.float32
BF16 = jnp.bfloat16

GX = 32
GY = 16
NZ = 16
ATOMS = 128
CH = 256
MODES = 512
SLOTS = 8
RADIAL = 64
SCALE = 1.0 / math.sqrt(33554432)
TURN = 2.0 * math.pi

PLANE_ORDER = (10, 9, 11, 6, 14, 8, 2, 5, 7, 13, 15, 4, 12, 1, 3)

COS_TERMS = [(-1.0) ** n * TURN ** (2 * n) / math.factorial(2 * n) for n in range(7)]

DISTANCES = [8 + 2 * q + k if k < 2 else 4 - 2 * q + k for q in range(4) for k in range(4)]
PLACE = [DISTANCES.index(d) for d in range(16)]


def halves(x):
    hi = x.astype(BF16)
    return hi, (x - hi.astype(F32)).astype(BF16)


def mm(a, b):
    return jnp.dot(a, b, preferred_element_type=F32)


def mm3(a_hi, a_lo, b_hi, b_lo):
    return mm(a_hi, b_hi) + (mm(a_hi, b_lo) + mm(a_lo, b_hi))


def cos_turns(turns):
    h = jnp.floor(turns * 2.0 + 0.5) * 0.5
    r = turns - h
    sign = 1.0 - 4.0 * (h - jnp.floor(h))
    y = r * r
    c = jnp.full_like(y, COS_TERMS[6])
    for n in range(5, -1, -1):
        c = c * y + COS_TERMS[n]
    return c * sign


def stacked(hi_lo, b_hi, b_lo):
    rows = hi_lo.shape[0] // 2
    upper = mm(hi_lo, b_hi)
    return upper[0:rows] + (upper[rows:] + mm(hi_lo[0:rows], b_lo))


def remote(src, dst, send, recv, gx, gy):
    return pltpu.make_async_remote_copy(
        src_ref=src, dst_ref=dst, send_sem=send, recv_sem=recv, device_id=(gx, gy), device_id_type=MESH
    )


def kernel(
    feat_h, offs_h, spec_h, neigh_h, mask_h, wv_h, vw_h, radw_h, emb_h, mixw_h, gf_h,
    out,
    feat, offs, spec, neigh, mask, wv, vw, embed, mixw, gf,
    near_pos, halo, tf, tt, ncol, wpad,
    part, theirs, got0, got1, sums, got2, rows16, own_row, filt1, filt2, filt3, rh_hi, rh_lo, lsum, lgot, last, tf_theirs, tt_theirs,
    dist, spj, rowid, onehot, bh, bl, filt, wcat, mix_hi, mix_lo, vb,
    ready, s_in, s_pair, r_pair, s_pos, r_pos, s_halo, r_halo, s_rs1, r_rs1, s_rs2, r_rs2, s_ag1, r_ag1, s_ag2, r_ag2, s_last, r_last,
):
    gx = lax.axis_index("gx")
    gy = lax.axis_index("gy")
    c = lax.rem(gx, 2)
    z = gx // 2
    px = gy // 4
    py = lax.rem(gy, 4)
    peer = gx + 1 - 2 * c
    other = lax.rem(gx + 31 + 2 * c, GX)
    up = lax.rem(gy + 1, GY)
    down = lax.rem(gy + GY - 1, GY)

    def plane(k):
        return lax.rem(px + k // 4, 4) * 4 + lax.rem(py + k % 4, 4)

    def column(k):
        return 2 * lax.rem(z + k, NZ) + c

    to_peer, to_other = 3 * (2 * c), 3 * (2 - 2 * c)
    around = [
        (peer, gy, to_peer + 1), (peer, up, to_peer), (peer, down, to_peer + 2),
        (other, gy, to_other + 1), (other, up, to_other), (other, down, to_other + 2),
        (gx, up, 3), (gx, down, 5),
    ]
    from_peer, from_other = to_other, to_peer
    slots_here = [
        from_peer + 1, from_peer, from_peer + 2, from_other + 1, from_other, from_other + 2, 3, 5,
    ]

    barrier = pltpu.get_barrier_semaphore()
    greeted = [(gx, plane(10)), (column(4), gy), (column(12), gy)]
    greeted += [(gx, plane(k)) for k in PLANE_ORDER[1:5]] + [(other, up), (other, down)]
    greeted += [(column(3), gy), (column(13), gy), (peer, up), (peer, down)]
    greeted += [(gx, plane(k)) for k in PLANE_ORDER[5:11]] + [(column(2), gy), (column(14), gy)]
    greeted += [(gx, plane(k)) for k in PLANE_ORDER[11:]] + [(column(1), gy), (column(15), gy)]
    greeted += [(other, gy), (peer, gy)]
    for device in greeted:
        pl.semaphore_signal(barrier, inc=1, device_id=device, device_id_type=MESH)

    loads = [
        pltpu.make_async_copy(src, dst, s_in.at[i])
        for i, (src, dst) in enumerate((
            (wv_h, wv), (offs_h.at[0], offs), (feat_h.at[0, 0], feat), (spec_h, spec), (vw_h, vw),
            (neigh_h.at[0, 0], neigh), (mask_h.at[0, 0], mask), (radw_h, embed.at[pl.ds(0, RADIAL)]),
            (emb_h, embed.at[pl.ds(RADIAL, RADIAL)]), (mixw_h, mixw), (gf_h.at[0], gf),
        ))
    ]
    for load in loads:
        load.start()
    for load in loads[0:4]:
        load.wait()
    near_pos[4] = jnp.zeros((8, ATOMS), F32)
    for i in range(3):
        near_pos[4, i:i + 1, :] = offs[i]
    near_pos[4, 3:4, :] = spec[0].astype(F32)

    wpad[...] = jnp.zeros(wpad.shape, F32)
    vectors = wv[...].astype(F32)
    wpad[0:3, :] = vectors
    even = wpad[0:8, :]
    odd = pltpu.roll(even, MODES - 16, 1)
    wpad[0:8, :] = jnp.where(c == 0, even, odd)
    wpad[8:16, :] = jnp.where(c == 0, odd, even)
    r = lax.broadcasted_iota(jnp.int32, (MODES, 1), 0)
    m = lax.broadcasted_iota(jnp.int32, (MODES, MODES), 1)
    q, k = r >> 7, r & 3
    away = jnp.where(k < 2, 8 + 2 * q, 4 - 2 * q) + k
    target = 32 * ((z + away) & 15) + ((r >> 3) & 15)
    pick = jnp.where(m == target, 1.0, 0.0).astype(BF16)
    ncol[...] = lax.dot_general(
        pick, wpad[...].astype(BF16), (((1,), (1,)), ((), ())), preferred_element_type=F32
    )

    def table(i, parity, block, positions):
        quarter = ((lax.broadcasted_iota(jnp.int32, (64, ATOMS), 0) >> 2) & 1).astype(F32) * 0.25
        rows = []
        for h in range(2):
            n = ncol[pl.ds(pl.multiple_of(i * 128 + h * 64, 64), 64), :]
            n0, n1, n2 = [n[:, 8 * parity + a:8 * parity + a + 1] for a in range(3)]
            w0 = (n0.astype(jnp.int32) * block & 31).astype(F32)
            w1 = (n1.astype(jnp.int32) * gy & 15).astype(F32)
            turns = (w0 + n0 * positions[0]) * (1.0 / 32)
            turns = turns + (w1 + n1 * positions[1]) * (1.0 / 16)
            turns = turns + n2 * positions[2]
            rows.append(cos_turns(turns - quarter))
        return jnp.concatenate(rows, axis=0)

    f_hi, f_lo = halves(feat[...])

    def own_table(i, parity, into):
        both = table(i, parity, gx, [offs[0], offs[1], offs[2]])
        t_hi, t_lo = halves(both)
        into[i] = mm3(t_hi, t_lo, f_hi, f_lo).reshape(16, 8, CH)
        return both

    def own_step(i, carry):
        tf_theirs[i] = own_table(i, 1, theirs)
        tf[i, :, 0:ATOMS] = own_table(i, 0, part)
        return carry

    lax.fori_loop(0, 4, own_step, 0)

    sends = []

    def start(src, dst, s_sems, r_sems, i, x, y):
        copy = remote(src, dst, s_sems.at[i], r_sems.at[i], x, y)
        copy.start()
        sends.append(copy)

    def start_all(copies, s_sems, r_sems, i, whole):
        for src, dst, x, y in copies:
            remote(src, dst, s_sems.at[i], r_sems.at[i], x, y).start()
        sends.append(remote(whole, whole, s_sems.at[i], r_sems.at[i], peer, gy))

    def arrived(dst, r_sems, i):
        remote(dst, dst, s_pair.at[0], r_sems.at[i], peer, gy).wait_recv()

    def drain():
        while sends:
            sends.pop(0).wait_send()

    pl.semaphore_wait(barrier, len(greeted))
    for q in range(4):
        start(theirs.at[q], got0.at[q], s_pair, r_pair, q, peer, gy)

    for k in (4, 12):
        pl.semaphore_signal(ready, inc=1, device_id=(column(k), gy), device_id_type=MESH)
    for i, (x, y, slot) in enumerate(around):
        start(near_pos.at[4], near_pos.at[slot], s_pos, r_pos, i, x, y)

    for q in range(4):
        arrived(got0.at[q], r_pair, q)
        part[q] = part[q] + got0[q]
        copies = [(part.at[q, plane(k)], got1.at[q, k], gx, plane(k)) for k in PLANE_ORDER]
        start_all(copies, s_rs1, r_rs1, q, got1.at[q, pl.ds(1, 15)])

    loads[4].wait()
    vw_hi, vw_lo = halves(vw[...])
    halo[4] = jnp.transpose(mm3(f_hi, f_lo, vw_hi, vw_lo))
    start(halo.at[4], halo.at[7 - 6 * c], s_halo, r_halo, 1, other, gy)
    start(halo.at[4], halo.at[1 + 6 * c], s_halo, r_halo, 0, peer, gy)
    pl.semaphore_wait(ready, 2)

    copies = []
    for q in range(4):
        arrived(got1.at[q, pl.ds(1, 15)], r_rs1, q)
        total = part[q, gy]
        for k in range(1, 16):
            total = total + got1[q, k]
        for k in range(4):
            sums[4 * q + k, 0:1, :] = total[k:k + 1, :]
            sums[4 * q + k, 1:2, :] = total[4 + k:5 + k, :]
        for k in (0, 1, 3, 2):
            d = DISTANCES[4 * q + k]
            if d:
                remote(
                    sums.at[4 * q + k], got2.at[d], s_rs2.at[0], r_rs2.at[0], column(d), gy
                ).start()
    sends.append(remote(got2.at[pl.ds(1, 15)], got2.at[pl.ds(1, 15)], s_rs2.at[0], r_rs2.at[0], peer, gy))

    arrived(halo.at[7 - 6 * c], r_halo, 0)
    arrived(halo.at[1 + 6 * c], r_halo, 1)
    for i in range(3):
        start(halo.at[3 * i + 1], halo.at[3 * i], s_halo, r_halo, 2 + i, gx, up)
        start(halo.at[3 * i + 1], halo.at[3 * i + 2], s_halo, r_halo, 5 + i, gx, down)

    for load in loads[5:]:
        load.wait()
    mine = lax.broadcasted_iota(jnp.int32, (3, MODES), 1) == gx * 16 + gy
    wave = jnp.sum(jnp.where(mine, vectors, 0.0), axis=1, keepdims=True)
    wave0 = wave[0:1] * (TURN / 32)
    wave1 = wave[1:2] * (TURN / 16)
    wave2 = wave[2:3] * TURN
    damp = jnp.exp(-0.01 * (wave0 * wave0 + wave1 * wave1 + wave2 * wave2)) * SCALE
    gf_hi, gf_lo = halves(gf[...])
    rows16[...] = jnp.zeros(rows16.shape, F32)

    for i, slot in enumerate(slots_here):
        arrived(near_pos.at[slot], r_pos, i)

    def peer_step(i, carry):
        there = near_pos[from_peer + 1]
        tf[i, :, ATOMS:2 * ATOMS] = table(i, 0, peer, [there[0:1], there[1:2], there[2:3]])
        return carry

    lax.fori_loop(0, 4, peer_step, 0)
    for i in range(4):
        hi, lo = halves(jnp.transpose(tf[i]))
        for at, rows in ((0, slice(ATOMS, 2 * ATOMS)), (2 * ATOMS, slice(0, ATOMS))):
            tt[i, at:at + ATOMS, :] = hi[rows]
            tt[i, at + ATOMS:at + 2 * ATOMS, :] = lo[rows]
    hi, lo = halves(jnp.transpose(tf_theirs[0]))
    tt_theirs[0:ATOMS] = hi
    tt_theirs[ATOMS:2 * ATOMS] = lo
    wt = jnp.transpose(embed[...])
    hi, lo = halves(wt)
    wcat[:, 0:128] = hi
    wcat[:, 128:256] = lo
    hi, lo = halves(jnp.transpose(mixw[...]))
    mix_hi[...] = hi
    mix_lo[...] = lo

    listed = jnp.where(mask[...] > 0, neigh[...], -1)
    source = listed >> 7
    atom = listed & 127
    s = (((source >> 4) - gx + 1) & 31) - 1
    t = (((source & 15) - gy + 1) & 15) - 1
    near = (s + 1) * 3 + (t + 1)
    rowid[...] = jnp.where(listed < 0, -1, near * ATOMS + atom)

    def onehot_step(e, carry):
        lanes = pl.ds(pl.multiple_of(e * ATOMS, ATOMS), ATOMS)
        place = rowid[pl.ds(e, 1), :]
        at = lax.broadcasted_iota(jnp.int32, (ATOMS, ATOMS), 0)
        for j in range(9):
            hit = jnp.where(at == place - ATOMS * j, 1.0, 0.0)
            onehot[ATOMS * j:ATOMS * j + ATOMS, lanes] = hit.astype(BF16)
        return carry

    lax.fori_loop(0, SLOTS, onehot_step, 0)

    found = [jnp.zeros((SLOTS, ATOMS), F32) for _ in range(4)]
    for j in range(9):
        for i in range(4):
            row = jnp.broadcast_to(near_pos[j, i:i + 1, :], (SLOTS, ATOMS))
            taken = jnp.take_along_axis(row, atom, axis=1)
            found[i] = jnp.where(near == j, taken, found[i])
    own = near_pos[4]
    gap0 = (s.astype(F32) + found[0]) - own[0:1, :]
    gap1 = (t.astype(F32) + found[1]) - own[1:2, :]
    gap2 = found[2] - own[2:3, :]
    dist[...] = jnp.sqrt(gap0 * gap0 + gap1 * gap1 + gap2 * gap2 + 0.01)
    spj[...] = found[3]
    own_kind = own[3:4, :]

    def basis_step(e, carry):
        lanes = pl.ds(pl.multiple_of(e * ATOMS, ATOMS), ATOMS)
        k = lax.broadcasted_iota(jnp.int32, (RADIAL, ATOMS), 0).astype(F32)
        scaled = (dist[pl.ds(e, 1), :] - k * (3.0 / 63)) / (6.0 / 63)
        hi, lo = halves(jnp.exp(-scaled * scaled))
        kinds = jnp.where(k == spj[pl.ds(e, 1), :], 1.0, 0.0) + jnp.where(k == own_kind, 1.0, 0.0)
        kinds = kinds.astype(BF16)
        bh[0:64, lanes] = hi
        bh[64:128, lanes] = kinds
        bh[128:192, lanes] = hi
        bh[192:256, lanes] = kinds
        bl[:, lanes] = lo
        return carry

    lax.fori_loop(0, SLOTS, basis_step, 0)

    def filter_step(e, carry):
        lanes = pl.ds(pl.multiple_of(e * 256, 256), 256)
        before = mm(wcat[...], bh[:, lanes]) + mm(wcat[:, 0:64], bl[:, lanes])
        hi, lo = halves(before / (1.0 + jnp.exp(-before)))
        filt[:, lanes] = mm3(mix_hi[...], mix_lo[...], hi, lo)
        return carry

    lax.fori_loop(0, 4, filter_step, 0)
    arrived(got2.at[pl.ds(1, 15)], r_rs2, 0)
    total = sums[PLACE[0]]
    for k in range(1, 16):
        total = total + got2[k]
    rows16[0:2, :] = total
    mixed = stacked(jnp.concatenate(halves(rows16[...]), axis=0), gf_hi, gf_lo)
    own_row[0] = mixed[0:2, :] * damp
    for d in (8, 7, 9, 6, 10, 5, 11, 4, 12, 3, 13, 2, 14, 1, 15):
        at = PLACE[16 - d]
        remote(own_row.at[0], filt1.at[at], s_ag1.at[0], r_ag1.at[at // 4], column(d), gy).start()
    sends.append(remote(got2.at[pl.ds(1, 15)], got2.at[pl.ds(1, 15)], s_ag1.at[0], r_ag1.at[0], peer, gy))

    drain()

    for q in (3, 2, 1, 0):
        arrived(filt1.at[pl.ds(4 * q, 4 if q < 3 else 3)], r_ag1, q)
        for k in range(4):
            at = 4 * q + k
            row = own_row.at[0] if at == PLACE[0] else filt1.at[at]
            filt2[q, k:k + 1, :] = row[0:1, :]
            filt2[q, 4 + k:5 + k, :] = row[1:2, :]
        copies = [(filt2.at[q], filt3.at[q, gy], gx, plane(k)) for k in PLANE_ORDER]
        start_all(copies, s_ag2, r_ag2, q, got1.at[q, pl.ds(1, 15)])
        if q == 0:
            copies = [(filt2.at[0], last.at[gy], peer, plane(k)) for k in PLANE_ORDER + (0,)]
            start_all(copies, s_last, r_last, 0, got1.at[0])
        filt3[q, gy] = filt2[q]

    for i in range(3):
        arrived(halo.at[3 * i], r_halo, 2 + i)
        arrived(halo.at[3 * i + 2], r_halo, 5 + i)
    for j in range(9):
        hi, lo = halves(halo[j])
        vb[0:CH, ATOMS * j:ATOMS * j + ATOMS] = hi
        vb[CH:2 * CH, ATOMS * j:ATOMS * j + ATOMS] = lo

    def gather_step(e, acc):
        lanes = pl.ds(pl.multiple_of(e * 256, 256), 256)
        g = mm(vb[...], onehot[:, lanes])
        msg = (g[0:CH] + g[CH:2 * CH]) * filt[:, lanes]
        return acc + (msg[:, 0:ATOMS] + msg[:, ATOMS:2 * ATOMS])

    short = lax.fori_loop(0, 4, gather_step, jnp.zeros((CH, ATOMS), F32))
    out[0, 0] = jnp.transpose(short) * (1.0 / math.sqrt(SLOTS))

    def factors(q):
        arrived(filt3.at[q, pl.ds(0, 15)], r_ag2, q)
        hi, lo = halves(filt3[q].reshape(128, CH))
        rh_hi[...] = hi
        rh_lo[...] = lo

    def terms(q, rows):
        return stacked(tt[q, rows], rh_hi[...], rh_lo[...])

    near_rows, far_rows = slice(2 * ATOMS, 4 * ATOMS), slice(0, 2 * ATOMS)
    for q in (3, 2, 1):
        factors(q)
        lsum[...] = terms(q, far_rows) + (lsum[...] if q < 3 else 0.0)
        out[0, 0] += terms(q, near_rows)
    start(lsum, lgot, s_pair, r_pair, 4, peer, gy)
    drain()
    arrived(lgot, r_pair, 4)
    out[0, 0] += lgot[...]
    factors(0)
    base = terms(0, near_rows)
    arrived(last, r_last, 0)
    hi, lo = halves(last[...].reshape(128, CH))
    out[0, 0] += base + stacked(tt_theirs[...], hi, lo)


def shards(features, offsets, species, neighbours, edge_mask, wavevectors, vw, radw, emb, mixw, gf):
    vmem = pl.BlockSpec(memory_space=pltpu.VMEM)
    hbm = pl.BlockSpec(memory_space=pltpu.HBM)
    dma = pltpu.SemaphoreType.DMA
    scratch = [
        pltpu.VMEM((ATOMS, CH), F32),
        pltpu.VMEM((3, 1, ATOMS), F32),
        pltpu.VMEM((1, 1, ATOMS), jnp.int32),
        pltpu.VMEM((SLOTS, ATOMS), jnp.int32),
        pltpu.VMEM((SLOTS, ATOMS), jnp.int32),
        pltpu.VMEM((3, MODES), jnp.int32),
        pltpu.VMEM((CH, CH), F32),
        pltpu.VMEM((2 * RADIAL, CH), F32),
        pltpu.VMEM((CH, CH), F32),
        pltpu.VMEM((CH, CH), F32),
        pltpu.VMEM((9, 8, ATOMS), F32),
        pltpu.VMEM((9, CH, ATOMS), F32),
        pltpu.VMEM((4, 128, 2 * ATOMS), F32),
        pltpu.VMEM((4, 4 * ATOMS, 128), BF16),
        pltpu.VMEM((MODES, 128), F32),
        pltpu.VMEM((128, MODES), F32),
        pltpu.VMEM((4, GY, 8, CH), F32),
        pltpu.VMEM((4, GY, 8, CH), F32),
        pltpu.VMEM((4, GY, 8, CH), F32),
        pltpu.VMEM((4, GY, 8, CH), F32),
        pltpu.VMEM((NZ, 2, CH), F32),
        pltpu.VMEM((NZ, 2, CH), F32),
        pltpu.VMEM((16, CH), F32),
        pltpu.VMEM((1, 2, CH), F32),
        pltpu.VMEM((NZ, 2, CH), F32),
        pltpu.VMEM((4, 8, CH), F32),
        pltpu.VMEM((4, GY, 8, CH), F32),
        pltpu.VMEM((128, CH), BF16),
        pltpu.VMEM((128, CH), BF16),
        pltpu.VMEM((ATOMS, CH), F32),
        pltpu.VMEM((ATOMS, CH), F32),
        pltpu.VMEM((GY, 8, CH), F32),
        pltpu.VMEM((4, 128, ATOMS), F32),
        pltpu.VMEM((2 * ATOMS, 128), BF16),
        pltpu.VMEM((SLOTS, ATOMS), F32),
        pltpu.VMEM((SLOTS, ATOMS), F32),
        pltpu.VMEM((SLOTS, ATOMS), jnp.int32),
        pltpu.VMEM((9 * ATOMS, SLOTS * ATOMS), BF16),
        pltpu.VMEM((256, SLOTS * ATOMS), BF16),
        pltpu.VMEM((64, SLOTS * ATOMS), BF16),
        pltpu.VMEM((CH, SLOTS * ATOMS), F32),
        pltpu.VMEM((CH, 256), BF16),
        pltpu.VMEM((CH, CH), BF16),
        pltpu.VMEM((CH, CH), BF16),
        pltpu.VMEM((2 * CH, 9 * ATOMS), BF16),
        pltpu.SemaphoreType.REGULAR,
        dma((11,)),
        dma((5,)), dma((5,)),
        dma((8,)), dma((8,)),
        dma((8,)), dma((8,)),
        dma((4,)), dma((4,)),
        dma((1,)), dma((1,)),
        dma((1,)), dma((4,)),
        dma((4,)), dma((4,)),
        dma((1,)), dma((1,)),
    ]
    return pl.pallas_call(
        kernel,
        out_shape=jax.ShapeDtypeStruct((1, 1, ATOMS, CH), F32),
        in_specs=[hbm] * 11,
        out_specs=vmem,
        scratch_shapes=scratch,
        compiler_params=pltpu.CompilerParams(
            collective_id=0, has_side_effects=True, vmem_limit_bytes=40 * 1024 * 1024
        ),
    )(*[pltpu.with_memory_space_constraint(x, pltpu.HBM) for x in (
        features, jnp.transpose(offsets, (0, 2, 1, 3)), species, jnp.swapaxes(neighbours, 2, 3),
        jnp.swapaxes(edge_mask, 2, 3), wavevectors, vw, radw, emb, mixw, gf,
    )])


def solution(mesh):
    block = P("gx", "gy", None, None)
    placed = (block, block, P("gx", "gy", None), block, block, P(), P(), P(), P(), P(), P("gx", None, None))
    return jax.shard_map(shards, mesh=mesh, in_specs=placed, out_specs=block, check_vma=False)
```

```python
import math

import jax
import jax.numpy as jnp
from jax import lax
from jax.experimental import pallas as pl
from jax.experimental.pallas import tpu as pltpu
from jax.sharding import PartitionSpec as P

MESH = pl.DeviceIdType.MESH
F32 = jnp.float32
BF16 = jnp.bfloat16

GX = 32
GY = 16
NZ = 16
ATOMS = 128
CH = 256
MODES = 512
SLOTS = 8
RADIAL = 64
SCALE = 1.0 / math.sqrt(33554432)
TURN = 2.0 * math.pi

PLANE_ORDER = (10, 9, 11, 6, 14, 8, 2, 5, 7, 13, 15, 4, 12, 1, 3)

COS_TERMS = [(-1.0) ** n * TURN ** (2 * n) / math.factorial(2 * n) for n in range(7)]

DISTANCES = [8 + 2 * q + k if k < 2 else 4 - 2 * q + k for q in range(4) for k in range(4)]
PLACE = [DISTANCES.index(d) for d in range(16)]


def halves(x):
    hi = x.astype(BF16)
    return hi, (x - hi.astype(F32)).astype(BF16)


def mm(a, b):
    return jnp.dot(a, b, preferred_element_type=F32)


def mm3(a_hi, a_lo, b_hi, b_lo):
    return mm(a_hi, b_hi) + (mm(a_hi, b_lo) + mm(a_lo, b_hi))


def cos_turns(turns):
    h = jnp.floor(turns * 2.0 + 0.5) * 0.5
    r = turns - h
    sign = 1.0 - 4.0 * (h - jnp.floor(h))
    y = r * r
    c = jnp.full_like(y, COS_TERMS[6])
    for n in range(5, -1, -1):
        c = c * y + COS_TERMS[n]
    return c * sign


def stacked(hi_lo, b_hi, b_lo):
    rows = hi_lo.shape[0] // 2
    upper = mm(hi_lo, b_hi)
    return upper[0:rows] + (upper[rows:] + mm(hi_lo[0:rows], b_lo))


def remote(src, dst, send, recv, gx, gy):
    return pltpu.make_async_remote_copy(
        src_ref=src, dst_ref=dst, send_sem=send, recv_sem=recv, device_id=(gx, gy), device_id_type=MESH
    )


def kernel(
    feat_h, offs_h, spec_h, neigh_h, mask_h, wv_h, vw_h, radw_h, emb_h, mixw_h, gf_h,
    out,
    feat, offs, spec, neigh, mask, wv, vw, embed, mixw, gf,
    near_pos, halo, tf, tt, ncol, wpad,
    part, theirs, got0, got1, sums, got2, rows16, own_row, filt1, filt2, filt3, rh_hi, rh_lo, lsum, lgot, last, tf_theirs, tt_theirs,
    dist, spj, rowid, onehot, bh, bl, filt, wcat, mix_hi, mix_lo, vb,
    ready, s_in, s_pair, r_pair, s_pos, r_pos, s_halo, r_halo, s_rs1, r_rs1, s_rs2, r_rs2, s_ag1, r_ag1, s_ag2, r_ag2, s_last, r_last,
):
    gx = lax.axis_index("gx")
    gy = lax.axis_index("gy")
    c = lax.rem(gx, 2)
    z = gx // 2
    px = gy // 4
    py = lax.rem(gy, 4)
    peer = gx + 1 - 2 * c
    other = lax.rem(gx + 31 + 2 * c, GX)
    up = lax.rem(gy + 1, GY)
    down = lax.rem(gy + GY - 1, GY)

    def plane(k):
        return lax.rem(px + k // 4, 4) * 4 + lax.rem(py + k % 4, 4)

    def column(k):
        return 2 * lax.rem(z + k, NZ) + c

    to_peer, to_other = 3 * (2 * c), 3 * (2 - 2 * c)
    around = [
        (peer, gy, to_peer + 1), (peer, up, to_peer), (peer, down, to_peer + 2),
        (other, gy, to_other + 1), (other, up, to_other), (other, down, to_other + 2),
        (gx, up, 3), (gx, down, 5),
    ]
    from_peer, from_other = to_other, to_peer
    slots_here = [
        from_peer + 1, from_peer, from_peer + 2, from_other + 1, from_other, from_other + 2, 3, 5,
    ]

    barrier = pltpu.get_barrier_semaphore()
    greeted = [(gx, plane(10)), (column(4), gy), (column(12), gy)]
    greeted += [(gx, plane(k)) for k in PLANE_ORDER[1:5]] + [(other, up), (other, down)]
    greeted += [(column(3), gy), (column(13), gy), (peer, up), (peer, down)]
    greeted += [(gx, plane(k)) for k in PLANE_ORDER[5:11]] + [(column(2), gy), (column(14), gy)]
    greeted += [(gx, plane(k)) for k in PLANE_ORDER[11:]] + [(column(1), gy), (column(15), gy)]
    greeted += [(other, gy), (peer, gy)]
    for device in greeted:
        pl.semaphore_signal(barrier, inc=1, device_id=device, device_id_type=MESH)

    loads = [
        pltpu.make_async_copy(src, dst, s_in.at[i])
        for i, (src, dst) in enumerate((
            (wv_h, wv), (offs_h.at[0], offs), (feat_h.at[0, 0], feat), (spec_h, spec), (vw_h, vw),
            (neigh_h.at[0, 0], neigh), (mask_h.at[0, 0], mask), (radw_h, embed.at[pl.ds(0, RADIAL)]),
            (emb_h, embed.at[pl.ds(RADIAL, RADIAL)]), (mixw_h, mixw), (gf_h.at[0], gf),
        ))
    ]
    for load in loads:
        load.start()
    for load in loads[0:4]:
        load.wait()
    near_pos[4] = jnp.zeros((8, ATOMS), F32)
    for i in range(3):
        near_pos[4, i:i + 1, :] = offs[i]
    near_pos[4, 3:4, :] = spec[0].astype(F32)

    wpad[...] = jnp.zeros(wpad.shape, F32)
    vectors = wv[...].astype(F32)
    wpad[0:3, :] = vectors
    even = wpad[0:8, :]
    odd = pltpu.roll(even, MODES - 16, 1)
    wpad[0:8, :] = jnp.where(c == 0, even, odd)
    wpad[8:16, :] = jnp.where(c == 0, odd, even)
    r = lax.broadcasted_iota(jnp.int32, (MODES, 1), 0)
    m = lax.broadcasted_iota(jnp.int32, (MODES, MODES), 1)
    q, k = r >> 7, r & 3
    away = jnp.where(k < 2, 8 + 2 * q, 4 - 2 * q) + k
    target = 32 * ((z + away) & 15) + ((r >> 3) & 15)
    pick = jnp.where(m == target, 1.0, 0.0).astype(BF16)
    ncol[...] = lax.dot_general(
        pick, wpad[...].astype(BF16), (((1,), (1,)), ((), ())), preferred_element_type=F32
    )

    def table(i, parity, block, positions):
        quarter = ((lax.broadcasted_iota(jnp.int32, (64, ATOMS), 0) >> 2) & 1).astype(F32) * 0.25
        rows = []
        for h in range(2):
            n = ncol[pl.ds(pl.multiple_of(i * 128 + h * 64, 64), 64), :]
            n0, n1, n2 = [n[:, 8 * parity + a:8 * parity + a + 1] for a in range(3)]
            w0 = (n0.astype(jnp.int32) * block & 31).astype(F32)
            w1 = (n1.astype(jnp.int32) * gy & 15).astype(F32)
            turns = (w0 + n0 * positions[0]) * (1.0 / 32)
            turns = turns + (w1 + n1 * positions[1]) * (1.0 / 16)
            turns = turns + n2 * positions[2]
            rows.append(cos_turns(turns - quarter))
        return jnp.concatenate(rows, axis=0)

    f_hi, f_lo = halves(feat[...])

    def own_table(i, parity, into):
        both = table(i, parity, gx, [offs[0], offs[1], offs[2]])
        t_hi, t_lo = halves(both)
        into[i] = mm3(t_hi, t_lo, f_hi, f_lo).reshape(16, 8, CH)
        return both

    def own_step(i, carry):
        tf_theirs[i] = own_table(i, 1, theirs)
        tf[i, :, 0:ATOMS] = own_table(i, 0, part)
        return carry

    lax.fori_loop(0, 4, own_step, 0)

    sends = []

    def start(src, dst, s_sems, r_sems, i, x, y):
        copy = remote(src, dst, s_sems.at[i], r_sems.at[i], x, y)
        copy.start()
        sends.append(copy)

    def start_all(copies, s_sems, r_sems, i, whole):
        for src, dst, x, y in copies:
            remote(src, dst, s_sems.at[i], r_sems.at[i], x, y).start()
        sends.append(remote(whole, whole, s_sems.at[i], r_sems.at[i], peer, gy))

    def arrived(dst, r_sems, i):
        remote(dst, dst, s_pair.at[0], r_sems.at[i], peer, gy).wait_recv()

    def drain():
        while sends:
            sends.pop(0).wait_send()

    pl.semaphore_wait(barrier, len(greeted))
    for q in range(4):
        start(theirs.at[q], got0.at[q], s_pair, r_pair, q, peer, gy)

    for k in (4, 12):
        pl.semaphore_signal(ready, inc=1, device_id=(column(k), gy), device_id_type=MESH)
    for i, (x, y, slot) in enumerate(around):
        start(near_pos.at[4], near_pos.at[slot], s_pos, r_pos, i, x, y)

    for q in range(4):
        arrived(got0.at[q], r_pair, q)
        part[q] = part[q] + got0[q]
        copies = [(part.at[q, plane(k)], got1.at[q, k], gx, plane(k)) for k in PLANE_ORDER]
        start_all(copies, s_rs1, r_rs1, q, got1.at[q, pl.ds(1, 15)])

    loads[4].wait()
    vw_hi, vw_lo = halves(vw[...])
    halo[4] = jnp.transpose(mm3(f_hi, f_lo, vw_hi, vw_lo))
    start(halo.at[4], halo.at[7 - 6 * c], s_halo, r_halo, 1, other, gy)
    start(halo.at[4], halo.at[1 + 6 * c], s_halo, r_halo, 0, peer, gy)
    pl.semaphore_wait(ready, 2)

    copies = []
    for q in range(4):
        arrived(got1.at[q, pl.ds(1, 15)], r_rs1, q)
        total = part[q, gy]
        for k in range(1, 16):
            total = total + got1[q, k]
        for k in range(4):
            sums[4 * q + k, 0:1, :] = total[k:k + 1, :]
            sums[4 * q + k, 1:2, :] = total[4 + k:5 + k, :]
        for k in (0, 1, 3, 2):
            d = DISTANCES[4 * q + k]
            if d:
                remote(
                    sums.at[4 * q + k], got2.at[d], s_rs2.at[0], r_rs2.at[0], column(d), gy
                ).start()
    sends.append(remote(got2.at[pl.ds(1, 15)], got2.at[pl.ds(1, 15)], s_rs2.at[0], r_rs2.at[0], peer, gy))

    arrived(halo.at[7 - 6 * c], r_halo, 0)
    arrived(halo.at[1 + 6 * c], r_halo, 1)
    for i in range(3):
        start(halo.at[3 * i + 1], halo.at[3 * i], s_halo, r_halo, 2 + i, gx, up)
        start(halo.at[3 * i + 1], halo.at[3 * i + 2], s_halo, r_halo, 5 + i, gx, down)

    for load in loads[5:]:
        load.wait()
    mine = lax.broadcasted_iota(jnp.int32, (3, MODES), 1) == gx * 16 + gy
    wave = jnp.sum(jnp.where(mine, vectors, 0.0), axis=1, keepdims=True)
    wave0 = wave[0:1] * (TURN / 32)
    wave1 = wave[1:2] * (TURN / 16)
    wave2 = wave[2:3] * TURN
    damp = jnp.exp(-0.01 * (wave0 * wave0 + wave1 * wave1 + wave2 * wave2)) * SCALE
    gf_hi, gf_lo = halves(gf[...])
    rows16[...] = jnp.zeros(rows16.shape, F32)

    for i, slot in enumerate(slots_here):
        arrived(near_pos.at[slot], r_pos, i)

    def peer_step(i, carry):
        there = near_pos[from_peer + 1]
        tf[i, :, ATOMS:2 * ATOMS] = table(i, 0, peer, [there[0:1], there[1:2], there[2:3]])
        return carry

    lax.fori_loop(0, 4, peer_step, 0)
    for i in range(4):
        hi, lo = halves(jnp.transpose(tf[i]))
        for at, rows in ((0, slice(ATOMS, 2 * ATOMS)), (2 * ATOMS, slice(0, ATOMS))):
            tt[i, at:at + ATOMS, :] = hi[rows]
            tt[i, at + ATOMS:at + 2 * ATOMS, :] = lo[rows]
    hi, lo = halves(jnp.transpose(tf_theirs[0]))
    tt_theirs[0:ATOMS] = hi
    tt_theirs[ATOMS:2 * ATOMS] = lo
    wt = jnp.transpose(embed[...])
    hi, lo = halves(wt)
    wcat[:, 0:128] = hi
    wcat[:, 128:256] = lo
    hi, lo = halves(jnp.transpose(mixw[...]))
    mix_hi[...] = hi
    mix_lo[...] = lo

    listed = jnp.where(mask[...] > 0, neigh[...], -1)
    source = listed >> 7
    atom = listed & 127
    s = (((source >> 4) - gx + 1) & 31) - 1
    t = (((source & 15) - gy + 1) & 15) - 1
    near = (s + 1) * 3 + (t + 1)
    rowid[...] = jnp.where(listed < 0, -1, near * ATOMS + atom)

    def onehot_step(e, carry):
        lanes = pl.ds(pl.multiple_of(e * ATOMS, ATOMS), ATOMS)
        place = rowid[pl.ds(e, 1), :]
        at = lax.broadcasted_iota(jnp.int32, (ATOMS, ATOMS), 0)
        for j in range(9):
            hit = jnp.where(at == place - ATOMS * j, 1.0, 0.0)
            onehot[ATOMS * j:ATOMS * j + ATOMS, lanes] = hit.astype(BF16)
        return carry

    lax.fori_loop(0, SLOTS, onehot_step, 0)

    found = [jnp.zeros((SLOTS, ATOMS), F32) for _ in range(4)]
    for j in range(9):
        for i in range(4):
            row = jnp.broadcast_to(near_pos[j, i:i + 1, :], (SLOTS, ATOMS))
            taken = jnp.take_along_axis(row, atom, axis=1)
            found[i] = jnp.where(near == j, taken, found[i])
    own = near_pos[4]
    gap0 = (s.astype(F32) + found[0]) - own[0:1, :]
    gap1 = (t.astype(F32) + found[1]) - own[1:2, :]
    gap2 = found[2] - own[2:3, :]
    dist[...] = jnp.sqrt(gap0 * gap0 + gap1 * gap1 + gap2 * gap2 + 0.01)
    spj[...] = found[3]
    own_kind = own[3:4, :]

    def basis_step(e, carry):
        lanes = pl.ds(pl.multiple_of(e * ATOMS, ATOMS), ATOMS)
        k = lax.broadcasted_iota(jnp.int32, (RADIAL, ATOMS), 0).astype(F32)
        scaled = (dist[pl.ds(e, 1), :] - k * (3.0 / 63)) / (6.0 / 63)
        hi, lo = halves(jnp.exp(-scaled * scaled))
        kinds = jnp.where(k == spj[pl.ds(e, 1), :], 1.0, 0.0) + jnp.where(k == own_kind, 1.0, 0.0)
        kinds = kinds.astype(BF16)
        bh[0:64, lanes] = hi
        bh[64:128, lanes] = kinds
        bh[128:192, lanes] = hi
        bh[192:256, lanes] = kinds
        bl[:, lanes] = lo
        return carry

    lax.fori_loop(0, SLOTS, basis_step, 0)

    def filter_step(e, carry):
        lanes = pl.ds(pl.multiple_of(e * 256, 256), 256)
        before = mm(wcat[...], bh[:, lanes]) + mm(wcat[:, 0:64], bl[:, lanes])
        hi, lo = halves(before / (1.0 + jnp.exp(-before)))
        filt[:, lanes] = mm3(mix_hi[...], mix_lo[...], hi, lo)
        return carry

    lax.fori_loop(0, 4, filter_step, 0)
    arrived(got2.at[pl.ds(1, 15)], r_rs2, 0)
    total = sums[PLACE[0]]
    for k in range(1, 16):
        total = total + got2[k]
    rows16[0:2, :] = total
    mixed = stacked(jnp.concatenate(halves(rows16[...]), axis=0), gf_hi, gf_lo)
    own_row[0] = mixed[0:2, :] * damp
    for d in (8, 7, 9, 6, 10, 5, 11, 4, 12, 3, 13, 2, 14, 1, 15):
        at = PLACE[16 - d]
        remote(own_row.at[0], filt1.at[at], s_ag1.at[0], r_ag1.at[at // 4], column(d), gy).start()
    sends.append(remote(got2.at[pl.ds(1, 15)], got2.at[pl.ds(1, 15)], s_ag1.at[0], r_ag1.at[0], peer, gy))

    drain()

    for q in (3, 2, 1, 0):
        arrived(filt1.at[pl.ds(4 * q, 4 if q < 3 else 3)], r_ag1, q)
        for k in range(4):
            at = 4 * q + k
            row = own_row.at[0] if at == PLACE[0] else filt1.at[at]
            filt2[q, k:k + 1, :] = row[0:1, :]
            filt2[q, 4 + k:5 + k, :] = row[1:2, :]
        for k in PLANE_ORDER:
            to = plane(k)
            remote(filt2.at[q], filt3.at[q, gy], s_ag2.at[q], r_ag2.at[q], gx, to).start()
            if q == 0:
                remote(filt2.at[0], last.at[gy], s_last.at[0], r_last.at[0], peer, to).start()
        if q == 0:
            remote(filt2.at[0], last.at[gy], s_last.at[0], r_last.at[0], peer, gy).start()
            sends.append(remote(got1.at[0], got1.at[0], s_last.at[0], r_last.at[0], peer, gy))
        whole = got1.at[q, pl.ds(1, 15)]
        sends.append(remote(whole, whole, s_ag2.at[q], r_ag2.at[q], peer, gy))
        filt3[q, gy] = filt2[q]

    for i in range(3):
        arrived(halo.at[3 * i], r_halo, 2 + i)
        arrived(halo.at[3 * i + 2], r_halo, 5 + i)
    for j in range(9):
        hi, lo = halves(halo[j])
        vb[0:CH, ATOMS * j:ATOMS * j + ATOMS] = hi
        vb[CH:2 * CH, ATOMS * j:ATOMS * j + ATOMS] = lo

    def gather_step(e, acc):
        lanes = pl.ds(pl.multiple_of(e * 256, 256), 256)
        g = mm(vb[...], onehot[:, lanes])
        msg = (g[0:CH] + g[CH:2 * CH]) * filt[:, lanes]
        return acc + (msg[:, 0:ATOMS] + msg[:, ATOMS:2 * ATOMS])

    short = lax.fori_loop(0, 4, gather_step, jnp.zeros((CH, ATOMS), F32))
    out[0, 0] = jnp.transpose(short) * (1.0 / math.sqrt(SLOTS))

    def factors(q):
        arrived(filt3.at[q, pl.ds(0, 15)], r_ag2, q)
        hi, lo = halves(filt3[q].reshape(128, CH))
        rh_hi[...] = hi
        rh_lo[...] = lo

    def terms(q, rows):
        return stacked(tt[q, rows], rh_hi[...], rh_lo[...])

    near_rows, far_rows = slice(2 * ATOMS, 4 * ATOMS), slice(0, 2 * ATOMS)
    for q in (3, 2, 1):
        factors(q)
        lsum[...] = terms(q, far_rows) + (lsum[...] if q < 3 else 0.0)
        out[0, 0] += terms(q, near_rows)
    start(lsum, lgot, s_pair, r_pair, 4, peer, gy)
    drain()
    arrived(lgot, r_pair, 4)
    out[0, 0] += lgot[...]
    factors(0)
    base = terms(0, near_rows)
    arrived(last, r_last, 0)
    hi, lo = halves(last[...].reshape(128, CH))
    out[0, 0] += base + stacked(tt_theirs[...], hi, lo)


def shards(features, offsets, species, neighbours, edge_mask, wavevectors, vw, radw, emb, mixw, gf):
    vmem = pl.BlockSpec(memory_space=pltpu.VMEM)
    hbm = pl.BlockSpec(memory_space=pltpu.HBM)
    dma = pltpu.SemaphoreType.DMA
    scratch = [
        pltpu.VMEM((ATOMS, CH), F32),
        pltpu.VMEM((3, 1, ATOMS), F32),
        pltpu.VMEM((1, 1, ATOMS), jnp.int32),
        pltpu.VMEM((SLOTS, ATOMS), jnp.int32),
        pltpu.VMEM((SLOTS, ATOMS), jnp.int32),
        pltpu.VMEM((3, MODES), jnp.int32),
        pltpu.VMEM((CH, CH), F32),
        pltpu.VMEM((2 * RADIAL, CH), F32),
        pltpu.VMEM((CH, CH), F32),
        pltpu.VMEM((CH, CH), F32),
        pltpu.VMEM((9, 8, ATOMS), F32),
        pltpu.VMEM((9, CH, ATOMS), F32),
        pltpu.VMEM((4, 128, 2 * ATOMS), F32),
        pltpu.VMEM((4, 4 * ATOMS, 128), BF16),
        pltpu.VMEM((MODES, 128), F32),
        pltpu.VMEM((128, MODES), F32),
        pltpu.VMEM((4, GY, 8, CH), F32),
        pltpu.VMEM((4, GY, 8, CH), F32),
        pltpu.VMEM((4, GY, 8, CH), F32),
        pltpu.VMEM((4, GY, 8, CH), F32),
        pltpu.VMEM((NZ, 2, CH), F32),
        pltpu.VMEM((NZ, 2, CH), F32),
        pltpu.VMEM((16, CH), F32),
        pltpu.VMEM((1, 2, CH), F32),
        pltpu.VMEM((NZ, 2, CH), F32),
        pltpu.VMEM((4, 8, CH), F32),
        pltpu.VMEM((4, GY, 8, CH), F32),
        pltpu.VMEM((128, CH), BF16),
        pltpu.VMEM((128, CH), BF16),
        pltpu.VMEM((ATOMS, CH), F32),
        pltpu.VMEM((ATOMS, CH), F32),
        pltpu.VMEM((GY, 8, CH), F32),
        pltpu.VMEM((4, 128, ATOMS), F32),
        pltpu.VMEM((2 * ATOMS, 128), BF16),
        pltpu.VMEM((SLOTS, ATOMS), F32),
        pltpu.VMEM((SLOTS, ATOMS), F32),
        pltpu.VMEM((SLOTS, ATOMS), jnp.int32),
        pltpu.VMEM((9 * ATOMS, SLOTS * ATOMS), BF16),
        pltpu.VMEM((256, SLOTS * ATOMS), BF16),
        pltpu.VMEM((64, SLOTS * ATOMS), BF16),
        pltpu.VMEM((CH, SLOTS * ATOMS), F32),
        pltpu.VMEM((CH, 256), BF16),
        pltpu.VMEM((CH, CH), BF16),
        pltpu.VMEM((CH, CH), BF16),
        pltpu.VMEM((2 * CH, 9 * ATOMS), BF16),
        pltpu.SemaphoreType.REGULAR,
        dma((11,)),
        dma((5,)), dma((5,)),
        dma((8,)), dma((8,)),
        dma((8,)), dma((8,)),
        dma((4,)), dma((4,)),
        dma((1,)), dma((1,)),
        dma((1,)), dma((4,)),
        dma((4,)), dma((4,)),
        dma((1,)), dma((1,)),
    ]
    return pl.pallas_call(
        kernel,
        out_shape=jax.ShapeDtypeStruct((1, 1, ATOMS, CH), F32),
        in_specs=[hbm] * 11,
        out_specs=vmem,
        scratch_shapes=scratch,
        compiler_params=pltpu.CompilerParams(
            collective_id=0, has_side_effects=True, vmem_limit_bytes=40 * 1024 * 1024
        ),
    )(*[pltpu.with_memory_space_constraint(x, pltpu.HBM) for x in (
        features, jnp.transpose(offsets, (0, 2, 1, 3)), species, jnp.swapaxes(neighbours, 2, 3),
        jnp.swapaxes(edge_mask, 2, 3), wavevectors, vw, radw, emb, mixw, gf,
    )])


def solution(mesh):
    block = P("gx", "gy", None, None)
    placed = (block, block, P("gx", "gy", None), block, block, P(), P(), P(), P(), P(), P("gx", None, None))
    return jax.shard_map(shards, mesh=mesh, in_specs=placed, out_specs=block, check_vma=False)
```
